32 devices in a mesh: ctx: 8 (over z, x), head: 4 (over y, core).
Axes of the slice: x: 2, y: 2, z: 4, core: 2. Of those that a mesh axis runs over, the one named last changes fastest.
Arguments:
- queries: bfloat16 [4, 1024, 1024], P(None, 'ctx', 'head'), may hold values from -45 to 45
- keys: bfloat16 [4, 1024, 1024], P(None, 'ctx', 'head'), may hold values from -6 to 6
- values: bfloat16 [4, 1024, 1024], P(None, 'ctx', 'head'), may hold values from -6 to 6
- out_weight: bfloat16 [1024, 2048], P(None, 'head'), may hold values from -0.1875 to 0.1875
- global_ids: int32 [4, 2], replicated, may hold values from 0 to 15, as said below
- rand_ids: int32 [4, 16, 4], P(None, 'ctx'), may hold values from 0 to 15, as said below
- rand_count: int32 [4, 16], P(None, 'ctx'), may hold values from 1 to 4
Outputs:
- output: bfloat16 [4, 1024, 2048], P(None, 'ctx', 'head')
The draws below stay inside these ranges and needn't reach their ends.
Inputs may be any that keep to these rules, and one draw needn't show every extreme that they name: `global_ids`: block ids; the 2 ids of one sequence are distinct. `rand_ids`: block ids of the same sequence. Taking together the 2 query blocks that each of the 4 sequences has on one index of ctx, at most 4 live slots name blocks held by any one index of ctx.
All inputs are finite; a program needn't handle non-finite values.
Results may differ from the reference program's by a relative error of at most 0.0056.
Values may be sent and summed in bfloat16 or wider, within the bound.
No kernel may reach another device: no remote copies, remote signals or barrier semaphores. Data moves between devices by JAX's collectives and lax.ppermute only.
A program may use at most 64 MiB of HBM per device.

```python
import jax
import jax.numpy as jnp
from jax import lax

D = 2048
HEADS = 8
HEAD_DIM = 128
BLOCK = 64
GLOB = 2
RMAX = 4
SEQ_DEV = 128
SEQS = 4
LEN = 1024
NB = 16
HW = 1024


def query_key_pair(key):
    folded = jax.random.fold_in(key, 7)
    key_query, key_keys = jax.random.split(folded, 2)
    full_shape = (SEQS, LEN, HEADS * HEAD_DIM)
    query_vals = jnp.clip(jax.random.normal(key_query, full_shape, jnp.float32), -6.0, 6.0)
    key_vals = jnp.clip(jax.random.normal(key_keys, full_shape, jnp.float32), -6.0, 6.0)
    return (query_vals, key_vals)


def draw_queries(key, part):
    return query_key_pair(key)[0].astype(jnp.bfloat16)


def draw_keys(key, part):
    return query_key_pair(key)[1].astype(jnp.bfloat16)


def draw_global_ids(key, part):
    folded = jax.random.fold_in(key, 23)
    orders = jax.vmap(lambda single: jax.random.permutation(single, NB))(jax.random.split(folded, SEQS))
    chosen = orders[:, :GLOB]
    edge_ids = jnp.where(jnp.arange(GLOB) == 0, NB - 1, jnp.where(jnp.arange(GLOB) == 1, 0, chosen[0]))
    edge_clash = (chosen[0][:, None] == jnp.array([NB - 1, 0])[None, :]).any(axis=1) & (jnp.arange(GLOB) >= 2)
    fallback = jnp.arange(GLOB) + 1
    first_row = jnp.where(edge_clash, fallback, edge_ids)
    chosen = jnp.where((jnp.arange(SEQS) == 0)[:, None], first_row[None, :], chosen)
    return chosen.astype(jnp.int32)


def block_lists(key):
    folded = jax.random.fold_in(key, 19)
    key_perm, key_within, key_heavy, key_forced, key_light = jax.random.split(folded, 5)
    devices = LEN // SEQ_DEV
    per_device = SEQ_DEV // BLOCK
    request_total = SEQS * per_device * RMAX
    orders = jax.vmap(lambda single: jax.random.permutation(single, devices))(jax.random.split(key_perm, devices))
    ascending = jnp.arange(devices, dtype=orders.dtype)
    orders = orders.at[0].set(devices - 1 - ascending)
    orders = orders.at[1].set(ascending)
    owners = orders[:, jnp.arange(request_total) % devices]
    within = jax.random.randint(key_within, (devices, request_total), 0, per_device)
    within = within.at[0, 0].set(per_device - 1)
    within = within.at[1, 0].set(0)
    block_ids = (owners * per_device + within).reshape(devices, SEQS, per_device, RMAX)
    block_ids = jnp.transpose(block_ids, (1, 0, 2, 3)).reshape(SEQS, devices * per_device, RMAX)
    heavy_dev = jax.random.randint(key_heavy, (devices,), 0, 8) == 0
    forced = jax.random.randint(key_forced, (), 0, devices)
    heavy_dev = heavy_dev | (jnp.arange(devices) == forced)
    light_counts = jax.random.randint(key_light, (SEQS, devices, per_device), 1, RMAX)
    live_counts = jnp.where(heavy_dev[None, :, None], RMAX, light_counts).reshape(SEQS, devices * per_device)
    return (block_ids.astype(jnp.int32), live_counts.astype(jnp.int32))


def draw_rand_ids(key, part):
    return block_lists(key)[0]


def draw_rand_count(key, part):
    return block_lists(key)[1]


def shard_levels(stream_key, extent, cuts, low, largest):
    level, own = 1.0, jax.random.fold_in(stream_key, 6)
    for axis_at, parts in cuts:
        heights = jnp.exp(jax.random.uniform(jax.random.fold_in(own, axis_at), (parts,), jnp.float32, low / len(cuts), largest / len(cuts)))
        level = level * jnp.repeat(heights, extent[axis_at] // parts).reshape([-1 if axis == axis_at else 1 for axis in range(len(extent))])
    return level


def scatter_about(own_key, dims, spread, most, cuts=(), held_as=jnp.bfloat16):
    values = spread * jax.random.normal(own_key, dims, jnp.float32)
    if cuts:
        values = values * shard_levels(own_key, dims, cuts, -0.22, 0.18)
    return jnp.clip(values, -most, most).astype(held_as)


def setup_inputs(seed: int = 0) -> dict:
    arg_keys = jax.random.split(jax.random.key(seed), 8)
    return {
        "queries": draw_queries(jax.random.fold_in(arg_keys[7], 71), 0),
        "keys": draw_keys(jax.random.fold_in(arg_keys[7], 71), 0),
        "values": scatter_about(arg_keys[2], (SEQS, LEN, HW), 1.0, 6.0, ((1, 8), (2, 4))),
        "out_weight": scatter_about(arg_keys[3], (HW, D), HW ** -0.5, 0.1875, ((1, 4),)),
        "global_ids": draw_global_ids(jax.random.fold_in(arg_keys[7], 71), 0),
        "rand_ids": draw_rand_ids(jax.random.fold_in(arg_keys[7], 71), 0),
        "rand_count": draw_rand_count(jax.random.fold_in(arg_keys[7], 71), 0),
    }


def attend_block(query_block, key_rows, value_rows, live_cols):
    score_scale = HEAD_DIM ** -0.5
    scores = jnp.einsum("qhd,khd->hqk", query_block.astype(jnp.float32), key_rows.astype(jnp.float32)) * score_scale
    masked = jnp.where(live_cols[None, None, :], scores, -1e30)
    row_peak = jnp.max(masked, axis=-1, keepdims=True)
    weights = jnp.where(live_cols[None, None, :], jnp.exp(masked - row_peak), 0.0)
    row_total = jnp.sum(weights, axis=-1)
    rounded = lax.optimization_barrier(weights.astype(jnp.bfloat16)).astype(jnp.float32)
    weighted = jnp.einsum("hqk,khd->qhd", rounded, value_rows.astype(jnp.float32))
    return (weighted / jnp.transpose(row_total)[:, :, None]).astype(jnp.bfloat16)


def reference(queries, keys, values, out_weight, global_ids, rand_ids, rand_count):
    block_count = queries.shape[1] // BLOCK
    outputs = []
    for seq_index in range(SEQS):
        query_blocks = queries[seq_index].reshape(block_count, BLOCK, HEADS, HEAD_DIM)
        key_blocks = keys[seq_index].reshape(block_count, BLOCK, HEADS, HEAD_DIM)
        value_blocks = values[seq_index].reshape(block_count, BLOCK, HEADS, HEAD_DIM)
        shared_ids = global_ids[seq_index].astype(jnp.int32)

        def one_block(operands, query_blocks=query_blocks, key_blocks=key_blocks, value_blocks=value_blocks, shared_ids=shared_ids):
            block_index, listed, listed_count = operands
            window_ids = jnp.stack([(block_index - 1) % block_count, block_index, (block_index + 1) % block_count]).astype(jnp.int32)
            chosen = jnp.concatenate([window_ids, shared_ids, listed.astype(jnp.int32)])
            key_rows = jnp.take(key_blocks, chosen, axis=0).reshape(-1, HEADS, HEAD_DIM)
            value_rows = jnp.take(value_blocks, chosen, axis=0).reshape(-1, HEADS, HEAD_DIM)
            live_slots = jnp.concatenate([jnp.ones((3 + GLOB,), jnp.bool_), jnp.arange(RMAX, dtype=jnp.int32) < listed_count])
            live_cols = jnp.repeat(live_slots, BLOCK)
            return attend_block(jnp.take(query_blocks, block_index, axis=0), key_rows, value_rows, live_cols)

        attended = lax.map(one_block, (jnp.arange(block_count, dtype=jnp.int32), rand_ids[seq_index], rand_count[seq_index]))
        flattened = attended.reshape(block_count * BLOCK, HEADS * HEAD_DIM)
        outputs.append(jnp.dot(flattened, out_weight, preferred_element_type=jnp.float32).astype(jnp.bfloat16))
    return jnp.stack(outputs)
```

```python
import functools

import jax
import jax.numpy as jnp
from jax import lax
from jax.experimental import pallas as pl
from jax.experimental.pallas import tpu as pltpu
from jax.sharding import PartitionSpec as P

HEAD_DIM = 128
BLOCK = 64
GLOB = 2
RMAX = 4


def with_halo(cells, sides, width):
    for axis, dim in sides:
        count = lax.axis_size(axis)
        head = lax.slice_in_dim(cells, 0, width, axis=dim)
        tail = lax.slice_in_dim(cells, cells.shape[dim] - width, cells.shape[dim], axis=dim)
        cells = jnp.concatenate(
            [
                lax.ppermute(tail, axis, [(i, (i + 1) % count) for i in range(count)]),
                cells,
                lax.ppermute(head, axis, [((i + 1) % count, i) for i in range(count)]),
            ],
            axis=dim,
        )
    return cells


def slot_table(slot_of, live_flat, slot_total):
    return (
        (slot_of[:, None] == jnp.arange(slot_total, dtype=jnp.int32)[None, :]) & live_flat[:, None]
    ).astype(jnp.int32)


def general_path(queries, keys, values, out_weight, global_ids, rand_ids, rand_count):
    seq_count, seq_rows, local_width = queries.shape
    blocks_here = seq_rows // BLOCK
    heads_here = local_width // HEAD_DIM
    cycle_size = lax.axis_size("ctx")
    my_index = lax.axis_index("ctx")
    request_count = seq_count * blocks_here * RMAX
    capacity = (request_count + cycle_size - 1) // cycle_size
    slot_total = cycle_size * capacity
    key_width = 3 + GLOB + RMAX
    score_scale = HEAD_DIM ** (-0.5)
    token_pairs = jnp.stack([keys, values], 0)
    block_pairs = jnp.stack(
        [
            keys.reshape(seq_count, blocks_here, BLOCK, local_width),
            values.reshape(seq_count, blocks_here, BLOCK, local_width),
        ],
        2,
    ).reshape(seq_count * blocks_here, 2, BLOCK, local_width)
    extended = with_halo(token_pairs, (("ctx", 2),), BLOCK)
    own_blocks = token_pairs.reshape(2, seq_count, blocks_here, BLOCK, local_width)
    shared_owner = global_ids // blocks_here
    shared_local = global_ids % blocks_here
    picker = (
        (shared_local[:, :, None] == jnp.arange(blocks_here, dtype=jnp.int32)[None, None, :])
        & (shared_owner == my_index)[:, :, None]
    ).astype(jnp.bfloat16)
    contribution = jnp.einsum(
        "sgj,xsjtf->xsgtf", picker, own_blocks, preferred_element_type=jnp.float32
    )
    shared_rows = lax.psum(contribution, "ctx").astype(jnp.bfloat16)
    slot_ids = jnp.arange(RMAX, dtype=jnp.int32)
    live_flat = (slot_ids[None, None, :] < rand_count[:, :, None]).reshape(-1)
    owners = (rand_ids // blocks_here).reshape(-1)
    seq_of = jnp.arange(seq_count, dtype=jnp.int32)[:, None, None]
    block_codes = (seq_of * blocks_here + rand_ids % blocks_here).reshape(-1)
    hit_owner = (
        (owners[:, None] == jnp.arange(cycle_size, dtype=jnp.int32)[None, :]) & live_flat[:, None]
    ).astype(jnp.int32)
    rank_within = jnp.sum((jnp.cumsum(hit_owner, axis=0) - hit_owner) * hit_owner, axis=1)
    slot_of = jnp.where(live_flat, owners * capacity + rank_within, 0)
    slot_hits = slot_table(slot_of, live_flat, slot_total)
    requests_out = (jnp.sum(slot_hits * (block_codes[:, None] + 1), axis=0) - 1).reshape(
        cycle_size, capacity
    )
    wanted_here = lax.all_to_all(requests_out, "ctx", split_axis=0, concat_axis=0, tiled=True)
    beside_all = extended.reshape(2, seq_count, blocks_here + 2, BLOCK, local_width)
    window_keys = jnp.stack(
        [beside_all[:, :, offset : offset + blocks_here] for offset in range(3)], 3
    )
    shared_wide = jnp.broadcast_to(
        shared_rows[:, :, None], (2, seq_count, blocks_here, GLOB, BLOCK, local_width)
    )
    local_keys = jnp.concatenate([window_keys, shared_wide], 3)
    query_view = queries.reshape(seq_count, blocks_here, BLOCK, heads_here, HEAD_DIM)
    payload = jnp.take(block_pairs, jnp.maximum(wanted_here, 0).reshape(-1), axis=0).reshape(
        cycle_size, capacity, 2, BLOCK, local_width
    )
    received = lax.all_to_all(payload, "ctx", split_axis=0, concat_axis=0, tiled=True)
    random_rows = jnp.take(received.reshape(slot_total, 2, BLOCK, local_width), slot_of, axis=0)
    random_rows = jnp.moveaxis(
        random_rows.reshape(seq_count, blocks_here, RMAX, 2, BLOCK, local_width), 3, 0
    )
    all_keys = jnp.concatenate([local_keys, random_rows], 3).reshape(
        2, seq_count, blocks_here, key_width * BLOCK, heads_here, HEAD_DIM
    )
    scores = (
        jnp.einsum(
            "sjqhd,sjkhd->sjhqk", query_view, all_keys[0], preferred_element_type=jnp.float32
        )
        * score_scale
    )
    live_slots = jnp.concatenate(
        [
            jnp.ones((seq_count, blocks_here, 3 + GLOB), jnp.bool_),
            slot_ids[None, None, :] < rand_count[:, :, None],
        ],
        2,
    )
    live_cols = jnp.repeat(live_slots, BLOCK, axis=2)[:, :, None, None, :]
    masked = jnp.where(live_cols, scores, -1e30)
    row_peak = jnp.max(masked, axis=-1, keepdims=True)
    weights = jnp.where(live_cols, jnp.exp(masked - row_peak), 0.0)
    row_total = jnp.sum(weights, axis=-1)
    weighted = jnp.einsum(
        "sjhqk,sjkhd->sjqhd",
        weights.astype(jnp.bfloat16),
        all_keys[1],
        preferred_element_type=jnp.float32,
    )
    attention = (
        (weighted / jnp.moveaxis(row_total, 2, 3)[..., None])
        .astype(jnp.bfloat16)
        .reshape(seq_count, seq_rows, local_width)
    )
    projected = jnp.einsum(
        "stf,fo->sto",
        lax.all_gather(attention, "head", axis=2, tiled=True),
        out_weight,
        preferred_element_type=jnp.float32,
    )
    return projected.astype(jnp.bfloat16)


def pack_kernel(me_ref, glob_ref, rand_ref, count_ref, q_ref, k_ref, v_ref, out_ref, *, ctx):
    seq = pl.program_id(0)
    me = me_ref[0]
    rows = q_ref.shape[1]
    blocks_here = rows // BLOCK
    blocks = ctx * blocks_here
    tiles = ctx * rows // HEAD_DIM
    heads = q_ref.shape[2] // HEAD_DIM
    key_block = (
        lax.broadcasted_iota(jnp.int32, (tiles, HEAD_DIM), 0) * HEAD_DIM
        + lax.broadcasted_iota(jnp.int32, (tiles, HEAD_DIM), 1)
    ) // BLOCK
    counts = []
    for j in range(blocks_here):
        block = me * blocks_here + j
        listed = [lax.rem(block + blocks - 1, blocks), block, lax.rem(block + 1, blocks)]
        listed += [glob_ref[seq, g] for g in range(GLOB)]
        listed += [
            jnp.where(r < count_ref[seq, j], rand_ref[seq, j, r], -1) for r in range(RMAX)
        ]
        counts.append(sum((key_block == one).astype(jnp.float32) for one in listed))
    counts = jnp.concatenate(counts, 0).astype(jnp.bfloat16)
    for h in range(heads):
        cols = slice(h * HEAD_DIM, (h + 1) * HEAD_DIM)
        out_ref[h, 0, 0:rows, :] = q_ref[0, :, cols]
        out_ref[h, 0, rows : 2 * rows, :] = k_ref[0, :, cols]
        out_ref[h, 0, 2 * rows : 3 * rows, :] = v_ref[0, :, cols]
        out_ref[h, 0, 3 * rows :, :] = counts


def attend_kernel(got_ref, out_ref, *, rows):
    ctx = got_ref.shape[0]
    blocks_here = rows // BLOCK
    tiles = ctx * rows // HEAD_DIM
    scale = HEAD_DIM ** (-0.5) * 1.4426950408889634
    keys = jnp.concatenate([got_ref[c, rows : 2 * rows, :] for c in range(ctx)], 0)
    values = jnp.concatenate([got_ref[c, 2 * rows : 3 * rows, :] for c in range(ctx)], 0)
    for c in range(ctx):
        counts = got_ref[c, 3 * rows :, :].astype(jnp.float32)
        bias = jnp.where(counts > 0, jnp.log2(jnp.maximum(counts, 1.0)), -1e30)
        scores = lax.dot_general(
            got_ref[c, 0:rows, :], keys, (((1,), (1,)), ((), ())), preferred_element_type=jnp.float32
        )
        wide = jnp.concatenate(
            [
                jnp.concatenate(
                    [
                        jnp.broadcast_to(bias[j * tiles + i : j * tiles + i + 1, :], (BLOCK, HEAD_DIM))
                        for i in range(tiles)
                    ],
                    1,
                )
                for j in range(blocks_here)
            ],
            0,
        )
        shifted = scores * scale + wide
        weights = jnp.exp2(shifted - jnp.max(shifted, axis=1, keepdims=True))
        total = jnp.sum(weights, axis=1, keepdims=True)
        weighted = jnp.dot(weights.astype(jnp.bfloat16), values, preferred_element_type=jnp.float32)
        out_ref[c] = (weighted / total).astype(jnp.bfloat16)


def project_kernel(group_ref, own_ref, core_ref, far_ref, far_core_ref, weight_ref, out_ref):
    group = group_ref[0]
    heads, tokens, _ = own_ref.shape
    depth = heads * HEAD_DIM
    total = None
    for flip, part in enumerate((own_ref, core_ref, far_ref, far_core_ref)):
        start = pl.multiple_of((group ^ flip) * depth, depth)
        features = jnp.concatenate([part[h] for h in range(heads)], 1)
        term = jnp.dot(features, weight_ref[pl.ds(start, depth), :], preferred_element_type=jnp.float32)
        total = term if total is None else total + term
    out_ref[...] = total.astype(jnp.bfloat16)


def pair_path(queries, keys, values, out_weight, global_ids, rand_ids, rand_count):
    seqs, rows, local_width = queries.shape
    heads = local_width // HEAD_DIM
    ctx = lax.axis_size("ctx")
    me = lax.axis_index("ctx").astype(jnp.int32).reshape(1)
    group = lax.axis_index("head").astype(jnp.int32).reshape(1)
    mask_rows = (rows // BLOCK) * (ctx * rows // HEAD_DIM)
    high = 3 * rows + mask_rows
    smem = pl.BlockSpec(memory_space=pltpu.SMEM)
    vmem = pl.BlockSpec(memory_space=pltpu.VMEM)
    token_spec = pl.BlockSpec((1, rows, local_width), lambda s: (s, 0, 0))
    packed = pl.pallas_call(
        functools.partial(pack_kernel, ctx=ctx),
        grid=(seqs,),
        in_specs=[smem, smem, smem, smem, token_spec, token_spec, token_spec],
        out_specs=pl.BlockSpec((heads, 1, high, HEAD_DIM), lambda s: (0, s, 0, 0)),
        out_shape=jax.ShapeDtypeStruct((heads, seqs, high, HEAD_DIM), jnp.bfloat16),
        name="pack",
    )(me, global_ids, rand_ids, rand_count, queries, keys, values)
    got = lax.all_to_all(
        packed.reshape(ctx, high, HEAD_DIM), "ctx", split_axis=0, concat_axis=0, tiled=True
    )
    attention = pl.pallas_call(
        functools.partial(attend_kernel, rows=rows),
        in_specs=[vmem],
        out_specs=vmem,
        out_shape=jax.ShapeDtypeStruct((ctx, rows, HEAD_DIM), jnp.bfloat16),
        compiler_params=pltpu.CompilerParams(vmem_limit_bytes=32 << 20),
        name="attend",
    )(got)
    own = lax.all_to_all(attention, "ctx", split_axis=0, concat_axis=0, tiled=True)
    own = own.reshape(heads, seqs * rows, HEAD_DIM)
    count = lax.axis_size("head")
    flip = lambda part, bit: lax.ppermute(part, "head", [(i, i ^ bit) for i in range(count)])
    core = flip(own, 1)
    far = flip(own, 2)
    far_core = flip(far, 1)
    projected = pl.pallas_call(
        project_kernel,
        in_specs=[smem] + [vmem] * 5,
        out_specs=vmem,
        out_shape=jax.ShapeDtypeStruct((seqs * rows, out_weight.shape[1]), jnp.bfloat16),
        compiler_params=pltpu.CompilerParams(vmem_limit_bytes=32 << 20),
        name="project",
    )(group, own, core, far, far_core, out_weight)
    return projected.reshape(seqs, rows, out_weight.shape[1])


def on_device(queries, keys, values, out_weight, global_ids, rand_ids, rand_count):
    seqs, rows, local_width = queries.shape
    pairs = seqs * (local_width // HEAD_DIM)
    if pairs == lax.axis_size("ctx") and lax.axis_size("head") == 4 and rows == 2 * BLOCK:
        path = pair_path
    else:
        path = general_path
    return path(queries, keys, values, out_weight, global_ids, rand_ids, rand_count)


def solution(mesh):
    placed = (
        P(None, "ctx", "head"),
        P(None, "ctx", "head"),
        P(None, "ctx", "head"),
        P(None, "head"),
        P(),
        P(None, "ctx", None),
        P(None, "ctx"),
    )
    return jax.shard_map(
        on_device, mesh=mesh, in_specs=placed, out_specs=P(None, "ctx", "head"), check_vma=False
    )
```

```python
import functools

import jax
import jax.numpy as jnp
from jax import lax
from jax.experimental import pallas as pl
from jax.experimental.pallas import tpu as pltpu
from jax.sharding import PartitionSpec as P

HEAD_DIM = 128
BLOCK = 64
GLOB = 2
RMAX = 4


def with_halo(cells, sides, width):
    for axis, dim in sides:
        count = lax.axis_size(axis)
        head = lax.slice_in_dim(cells, 0, width, axis=dim)
        tail = lax.slice_in_dim(cells, cells.shape[dim] - width, cells.shape[dim], axis=dim)
        cells = jnp.concatenate(
            [
                lax.ppermute(tail, axis, [(i, (i + 1) % count) for i in range(count)]),
                cells,
                lax.ppermute(head, axis, [((i + 1) % count, i) for i in range(count)]),
            ],
            axis=dim,
        )
    return cells


def slot_table(slot_of, live_flat, slot_total):
    return (
        (slot_of[:, None] == jnp.arange(slot_total, dtype=jnp.int32)[None, :]) & live_flat[:, None]
    ).astype(jnp.int32)


def general_path(queries, keys, values, out_weight, global_ids, rand_ids, rand_count):
    seq_count, seq_rows, local_width = queries.shape
    blocks_here = seq_rows // BLOCK
    heads_here = local_width // HEAD_DIM
    cycle_size = lax.axis_size("ctx")
    my_index = lax.axis_index("ctx")
    request_count = seq_count * blocks_here * RMAX
    capacity = (request_count + cycle_size - 1) // cycle_size
    slot_total = cycle_size * capacity
    key_width = 3 + GLOB + RMAX
    score_scale = HEAD_DIM ** (-0.5)
    token_pairs = jnp.stack([keys, values], 0)
    block_pairs = jnp.stack(
        [
            keys.reshape(seq_count, blocks_here, BLOCK, local_width),
            values.reshape(seq_count, blocks_here, BLOCK, local_width),
        ],
        2,
    ).reshape(seq_count * blocks_here, 2, BLOCK, local_width)
    extended = with_halo(token_pairs, (("ctx", 2),), BLOCK)
    own_blocks = token_pairs.reshape(2, seq_count, blocks_here, BLOCK, local_width)
    shared_owner = global_ids // blocks_here
    shared_local = global_ids % blocks_here
    picker = (
        (shared_local[:, :, None] == jnp.arange(blocks_here, dtype=jnp.int32)[None, None, :])
        & (shared_owner == my_index)[:, :, None]
    ).astype(jnp.bfloat16)
    contribution = jnp.einsum(
        "sgj,xsjtf->xsgtf", picker, own_blocks, preferred_element_type=jnp.float32
    )
    shared_rows = lax.psum(contribution, "ctx").astype(jnp.bfloat16)
    slot_ids = jnp.arange(RMAX, dtype=jnp.int32)
    live_flat = (slot_ids[None, None, :] < rand_count[:, :, None]).reshape(-1)
    owners = (rand_ids // blocks_here).reshape(-1)
    seq_of = jnp.arange(seq_count, dtype=jnp.int32)[:, None, None]
    block_codes = (seq_of * blocks_here + rand_ids % blocks_here).reshape(-1)
    hit_owner = (
        (owners[:, None] == jnp.arange(cycle_size, dtype=jnp.int32)[None, :]) & live_flat[:, None]
    ).astype(jnp.int32)
    rank_within = jnp.sum((jnp.cumsum(hit_owner, axis=0) - hit_owner) * hit_owner, axis=1)
    slot_of = jnp.where(live_flat, owners * capacity + rank_within, 0)
    slot_hits = slot_table(slot_of, live_flat, slot_total)
    requests_out = (jnp.sum(slot_hits * (block_codes[:, None] + 1), axis=0) - 1).reshape(
        cycle_size, capacity
    )
    wanted_here = lax.all_to_all(requests_out, "ctx", split_axis=0, concat_axis=0, tiled=True)
    beside_all = extended.reshape(2, seq_count, blocks_here + 2, BLOCK, local_width)
    window_keys = jnp.stack(
        [beside_all[:, :, offset : offset + blocks_here] for offset in range(3)], 3
    )
    shared_wide = jnp.broadcast_to(
        shared_rows[:, :, None], (2, seq_count, blocks_here, GLOB, BLOCK, local_width)
    )
    local_keys = jnp.concatenate([window_keys, shared_wide], 3)
    query_view = queries.reshape(seq_count, blocks_here, BLOCK, heads_here, HEAD_DIM)
    payload = jnp.take(block_pairs, jnp.maximum(wanted_here, 0).reshape(-1), axis=0).reshape(
        cycle_size, capacity, 2, BLOCK, local_width
    )
    received = lax.all_to_all(payload, "ctx", split_axis=0, concat_axis=0, tiled=True)
    random_rows = jnp.take(received.reshape(slot_total, 2, BLOCK, local_width), slot_of, axis=0)
    random_rows = jnp.moveaxis(
        random_rows.reshape(seq_count, blocks_here, RMAX, 2, BLOCK, local_width), 3, 0
    )
    all_keys = jnp.concatenate([local_keys, random_rows], 3).reshape(
        2, seq_count, blocks_here, key_width * BLOCK, heads_here, HEAD_DIM
    )
    scores = (
        jnp.einsum(
            "sjqhd,sjkhd->sjhqk", query_view, all_keys[0], preferred_element_type=jnp.float32
        )
        * score_scale
    )
    live_slots = jnp.concatenate(
        [
            jnp.ones((seq_count, blocks_here, 3 + GLOB), jnp.bool_),
            slot_ids[None, None, :] < rand_count[:, :, None],
        ],
        2,
    )
    live_cols = jnp.repeat(live_slots, BLOCK, axis=2)[:, :, None, None, :]
    masked = jnp.where(live_cols, scores, -1e30)
    row_peak = jnp.max(masked, axis=-1, keepdims=True)
    weights = jnp.where(live_cols, jnp.exp(masked - row_peak), 0.0)
    row_total = jnp.sum(weights, axis=-1)
    weighted = jnp.einsum(
        "sjhqk,sjkhd->sjqhd",
        weights.astype(jnp.bfloat16),
        all_keys[1],
        preferred_element_type=jnp.float32,
    )
    attention = (
        (weighted / jnp.moveaxis(row_total, 2, 3)[..., None])
        .astype(jnp.bfloat16)
        .reshape(seq_count, seq_rows, local_width)
    )
    projected = jnp.einsum(
        "stf,fo->sto",
        lax.all_gather(attention, "head", axis=2, tiled=True),
        out_weight,
        preferred_element_type=jnp.float32,
    )
    return projected.astype(jnp.bfloat16)


NEAR = (1, 2, 3)
FAR = (4, 6, 5, 7)
EARLY, LATE = FAR[:2], FAR[2:]


def pack_kernel(me_ref, glob_ref, rand_ref, count_ref, q_ref, k_ref, v_ref, *outs, ctx):
    seqs, rows, width = q_ref.shape
    me = me_ref[0]
    blocks_here = rows // BLOCK
    blocks = ctx * blocks_here
    tiles = ctx * rows // HEAD_DIM
    mask_rows = blocks_here * tiles
    tile = lax.broadcasted_iota(jnp.int32, (tiles, HEAD_DIM), 0)
    lane = lax.broadcasted_iota(jnp.int32, (tiles, HEAD_DIM), 1)
    for flip, out in zip(FAR + NEAR + (0,), outs):
        asker = me ^ flip
        seq = lax.rem(asker, seqs)
        at = out.shape[0] - 2 * rows
        out[at : at + rows, :] = k_ref[seq]
        out[at + rows :, :] = v_ref[seq]
        if not at:
            continue
        out[0:rows, :] = q_ref[seq]
        key_block = ((tile ^ asker) * HEAD_DIM + lane) // BLOCK
        counts = []
        for j in range(blocks_here):
            block = me * blocks_here + j
            listed = [lax.rem(block + blocks - 1, blocks), block, lax.rem(block + 1, blocks)]
            listed += [glob_ref[g, seq] for g in range(GLOB)]
            listed += [
                jnp.where(r < count_ref[j, seq], rand_ref[seq, j, r], -1) for r in range(RMAX)
            ]
            counts.append(sum((key_block == one).astype(jnp.float32) for one in listed))
        counts = jnp.concatenate(counts, 0).astype(jnp.bfloat16)
        for h in range(width // HEAD_DIM):
            out[rows : rows + mask_rows, h * HEAD_DIM : (h + 1) * HEAD_DIM] = counts


def scores_of(asker, holders, flips, cols, rows, tiles):
    blocks_here = rows // BLOCK
    mask_rows = blocks_here * tiles
    scale = HEAD_DIM ** (-0.5) * 1.4426950408889634
    keys = [ref[ref.shape[0] - 2 * rows : ref.shape[0] - rows, cols] for ref in holders]
    scores = lax.dot_general(
        asker[0:rows, cols],
        jnp.concatenate(keys, 0),
        (((1,), (1,)), ((), ())),
        preferred_element_type=jnp.float32,
    )
    counts = asker[rows : rows + mask_rows, 0:HEAD_DIM].astype(jnp.float32)
    bias = jnp.where(counts > 0, jnp.log2(jnp.maximum(counts, 1.0)), -1e30)
    wide = jnp.concatenate(
        [
            jnp.concatenate(
                [
                    jnp.broadcast_to(bias[j * tiles + i : j * tiles + i + 1, :], (BLOCK, HEAD_DIM))
                    for i in flips
                ],
                1,
            )
            for j in range(blocks_here)
        ],
        0,
    )
    return scores * scale + wide


def weigh(weights, holders, cols, rows):
    values = [ref[ref.shape[0] - rows :, cols] for ref in holders]
    return jnp.dot(
        weights.astype(jnp.bfloat16), jnp.concatenate(values, 0), preferred_element_type=jnp.float32
    )


def near_kernel(*refs, rows, tiles, flips):
    *holders, out_ref = refs
    askers = holders[: len(holders) - len(flips)]
    heads = askers[0].shape[1] // HEAD_DIM
    for n, asker in enumerate(askers):
        for h in range(heads):
            cols = slice(h * HEAD_DIM, (h + 1) * HEAD_DIM)
            shifted = scores_of(asker, holders, tuple(range(len(askers))) + flips, cols, rows, tiles)
            peak = jnp.max(shifted, axis=1, keepdims=True)
            weights = jnp.exp2(shifted - peak)
            full = (rows, HEAD_DIM)
            out_ref[0, n * heads + h] = weigh(weights, holders, cols, rows)
            out_ref[1, n * heads + h] = jnp.broadcast_to(peak, full)
            out_ref[2, n * heads + h] = jnp.broadcast_to(jnp.sum(weights, axis=1, keepdims=True), full)


def far_kernel(me_ref, *refs, rows, tiles, flips, copies):
    *askers, before, out_ref = refs
    askers, holders = askers[: -len(flips)], askers[-len(flips) :]
    heads = askers[0].shape[1] // HEAD_DIM
    spot = lax.rem(me_ref[0], len(askers))
    for n, asker in enumerate(askers):
        for h in range(heads):
            cols = slice(h * HEAD_DIM, (h + 1) * HEAD_DIM)
            shifted = scores_of(asker, holders, flips, cols, rows, tiles)
            old = before[1, n * heads + h]
            peak = jnp.maximum(old, jnp.max(shifted, axis=1, keepdims=True))
            weights = jnp.exp2(shifted - jnp.concatenate([peak] * len(flips), 1))
            keep = jnp.exp2(old - peak)
            total = keep * before[2, n * heads + h] + jnp.sum(weights, axis=1, keepdims=True)
            weighted = keep * before[0, n * heads + h] + weigh(weights, holders, cols, rows)
            result = (weighted / total).astype(jnp.bfloat16)
            for copy in range(copies):
                out_ref[(spot ^ n) * copies + copy, :, cols] = result


def project_kernel(group_ref, *refs, flip):
    *before, part_ref, weight_ref, out_ref = refs
    slots, rows, depth = part_ref.shape
    seqs = out_ref.shape[0]
    sides = slots // seqs
    core = lax.rem(group_ref[0], weight_ref.shape[0] // (depth * sides)) ^ flip
    weights = [
        weight_ref[pl.ds(pl.multiple_of((side * sides + core) * depth, depth), depth), :]
        for side in range(sides)
    ]
    for seq in range(seqs):
        total = before[0][seq] if before else 0.0
        for side in range(sides):
            total = total + jnp.dot(
                part_ref[seq * sides + side], weights[side], preferred_element_type=jnp.float32
            )
        out_ref[seq] = total.astype(out_ref.dtype)


def half_path(queries, keys, values, out_weight, global_ids, rand_ids, rand_count):
    seqs, rows, local_width = queries.shape
    ctx = lax.axis_size("ctx")
    groups = lax.axis_size("head")
    me = lax.axis_index("ctx").astype(jnp.int32).reshape(1)
    group = lax.axis_index("head").astype(jnp.int32).reshape(1)
    heads = local_width // HEAD_DIM
    tiles = ctx * rows // HEAD_DIM
    mask_rows = rows // BLOCK * tiles
    smem = pl.BlockSpec(memory_space=pltpu.SMEM)
    vmem = pl.BlockSpec(memory_space=pltpu.VMEM)
    room = pltpu.CompilerParams(vmem_limit_bytes=32 << 20)
    tall = lambda high: jax.ShapeDtypeStruct((high, local_width), jnp.bfloat16)
    shapes = [tall(2 * rows)] * len(FAR) + [tall(3 * rows + mask_rows)] * (len(NEAR) + 1)
    *sent, own = pl.pallas_call(
        functools.partial(pack_kernel, ctx=ctx),
        in_specs=[smem] * 4 + [vmem] * 3,
        out_specs=[vmem] * len(shapes),
        out_shape=shapes,
        name="pack",
    )(me, global_ids.T, rand_ids, rand_count.T, queries, keys, values)
    sent = dict(zip(FAR + NEAR, sent))
    got = {
        flip: lax.ppermute(sent[flip], "ctx", [(i, i ^ flip) for i in range(ctx)])
        for flip in (1, 4, 6, 2, 5, 3, 7)
    }
    near = [own] + [got[flip] for flip in NEAR]
    pairs = heads * (seqs * rows) ** 2
    cost = pl.CostEstimate(
        flops=4 * pairs * HEAD_DIM, bytes_accessed=8 * seqs * rows * local_width, transcendentals=pairs
    )
    so_far = pl.pallas_call(
        functools.partial(near_kernel, rows=rows, tiles=tiles, flips=EARLY),
        in_specs=[vmem] * (len(near) + len(EARLY)),
        out_specs=vmem,
        out_shape=jax.ShapeDtypeStruct((3, seqs * heads, rows, HEAD_DIM), jnp.float32),
        compiler_params=room,
        cost_estimate=cost,
        name="attend_near",
    )(*near, *[got[flip] for flip in EARLY])
    sides = 2
    attention = pl.pallas_call(
        functools.partial(far_kernel, rows=rows, tiles=tiles, flips=LATE, copies=sides),
        in_specs=[smem] + [vmem] * (len(near) + len(LATE) + 1),
        out_specs=vmem,
        out_shape=jax.ShapeDtypeStruct((seqs * sides, rows, local_width), jnp.bfloat16),
        compiler_params=room,
        cost_estimate=cost,
        name="attend_far",
    )(me, *near, *[got[flip] for flip in LATE], so_far)
    cores = groups // sides
    home = lax.all_to_all(
        attention,
        ("ctx", "head"),
        split_axis=0,
        concat_axis=0,
        tiled=True,
        axis_index_groups=[
            [(half * seqs + c) * groups + side * cores + core for c in range(seqs) for side in range(sides)]
            for half in range(ctx // seqs)
            for core in range(cores)
        ],
    )
    beside = lax.ppermute(home, "head", [(i, i ^ 1) for i in range(groups)])
    width = out_weight.shape[1]

    def project(flip, dtype, *parts):
        return pl.pallas_call(
            functools.partial(project_kernel, flip=flip),
            in_specs=[smem] + [vmem] * (len(parts) + 1),
            out_specs=vmem,
            out_shape=jax.ShapeDtypeStruct((seqs, rows, width), dtype),
            compiler_params=room,
            cost_estimate=pl.CostEstimate(
                flops=seqs * rows * width * out_weight.shape[0],
                bytes_accessed=4 * seqs * rows * width,
                transcendentals=0,
            ),
            name="project",
        )(group, *parts, out_weight)

    return project(1, jnp.bfloat16, project(0, jnp.float32, home), beside)


def on_device(queries, keys, values, out_weight, global_ids, rand_ids, rand_count):
    seqs, rows, local_width = queries.shape
    ctx, groups = lax.axis_size("ctx"), lax.axis_size("head")
    fits = ctx == 2 * seqs == 8 and groups == 4 and rows == HEAD_DIM == 2 * BLOCK
    path = half_path if fits else general_path
    return path(queries, keys, values, out_weight, global_ids, rand_ids, rand_count)


def solution(mesh):
    placed = (
        P(None, "ctx", "head"),
        P(None, "ctx", "head"),
        P(None, "ctx", "head"),
        P(None, "head"),
        P(),
        P(None, "ctx", None),
        P(None, "ctx"),
    )
    return jax.shard_map(
        on_device, mesh=mesh, in_specs=placed, out_specs=P(None, "ctx", "head"), check_vma=False
    )
```

```python
import functools

import jax
import jax.numpy as jnp
from jax import lax
from jax.experimental import pallas as pl
from jax.experimental.pallas import tpu as pltpu
from jax.sharding import PartitionSpec as P

HEAD_DIM = 128
BLOCK = 64
GLOB = 2
RMAX = 4


def with_halo(cells, sides, width):
    for axis, dim in sides:
        count = lax.axis_size(axis)
        head = lax.slice_in_dim(cells, 0, width, axis=dim)
        tail = lax.slice_in_dim(cells, cells.shape[dim] - width, cells.shape[dim], axis=dim)
        cells = jnp.concatenate(
            [
                lax.ppermute(tail, axis, [(i, (i + 1) % count) for i in range(count)]),
                cells,
                lax.ppermute(head, axis, [((i + 1) % count, i) for i in range(count)]),
            ],
            axis=dim,
        )
    return cells


def slot_table(slot_of, live_flat, slot_total):
    return (
        (slot_of[:, None] == jnp.arange(slot_total, dtype=jnp.int32)[None, :]) & live_flat[:, None]
    ).astype(jnp.int32)


def general_path(queries, keys, values, out_weight, global_ids, rand_ids, rand_count):
    seq_count, seq_rows, local_width = queries.shape
    blocks_here = seq_rows // BLOCK
    heads_here = local_width // HEAD_DIM
    cycle_size = lax.axis_size("ctx")
    my_index = lax.axis_index("ctx")
    request_count = seq_count * blocks_here * RMAX
    capacity = (request_count + cycle_size - 1) // cycle_size
    slot_total = cycle_size * capacity
    key_width = 3 + GLOB + RMAX
    score_scale = HEAD_DIM ** (-0.5)
    token_pairs = jnp.stack([keys, values], 0)
    block_pairs = jnp.stack(
        [
            keys.reshape(seq_count, blocks_here, BLOCK, local_width),
            values.reshape(seq_count, blocks_here, BLOCK, local_width),
        ],
        2,
    ).reshape(seq_count * blocks_here, 2, BLOCK, local_width)
    extended = with_halo(token_pairs, (("ctx", 2),), BLOCK)
    own_blocks = token_pairs.reshape(2, seq_count, blocks_here, BLOCK, local_width)
    shared_owner = global_ids // blocks_here
    shared_local = global_ids % blocks_here
    picker = (
        (shared_local[:, :, None] == jnp.arange(blocks_here, dtype=jnp.int32)[None, None, :])
        & (shared_owner == my_index)[:, :, None]
    ).astype(jnp.bfloat16)
    contribution = jnp.einsum(
        "sgj,xsjtf->xsgtf", picker, own_blocks, preferred_element_type=jnp.float32
    )
    shared_rows = lax.psum(contribution, "ctx").astype(jnp.bfloat16)
    slot_ids = jnp.arange(RMAX, dtype=jnp.int32)
    live_flat = (slot_ids[None, None, :] < rand_count[:, :, None]).reshape(-1)
    owners = (rand_ids // blocks_here).reshape(-1)
    seq_of = jnp.arange(seq_count, dtype=jnp.int32)[:, None, None]
    block_codes = (seq_of * blocks_here + rand_ids % blocks_here).reshape(-1)
    hit_owner = (
        (owners[:, None] == jnp.arange(cycle_size, dtype=jnp.int32)[None, :]) & live_flat[:, None]
    ).astype(jnp.int32)
    rank_within = jnp.sum((jnp.cumsum(hit_owner, axis=0) - hit_owner) * hit_owner, axis=1)
    slot_of = jnp.where(live_flat, owners * capacity + rank_within, 0)
    slot_hits = slot_table(slot_of, live_flat, slot_total)
    requests_out = (jnp.sum(slot_hits * (block_codes[:, None] + 1), axis=0) - 1).reshape(
        cycle_size, capacity
    )
    wanted_here = lax.all_to_all(requests_out, "ctx", split_axis=0, concat_axis=0, tiled=True)
    beside_all = extended.reshape(2, seq_count, blocks_here + 2, BLOCK, local_width)
    window_keys = jnp.stack(
        [beside_all[:, :, offset : offset + blocks_here] for offset in range(3)], 3
    )
    shared_wide = jnp.broadcast_to(
        shared_rows[:, :, None], (2, seq_count, blocks_here, GLOB, BLOCK, local_width)
    )
    local_keys = jnp.concatenate([window_keys, shared_wide], 3)
    query_view = queries.reshape(seq_count, blocks_here, BLOCK, heads_here, HEAD_DIM)
    payload = jnp.take(block_pairs, jnp.maximum(wanted_here, 0).reshape(-1), axis=0).reshape(
        cycle_size, capacity, 2, BLOCK, local_width
    )
    received = lax.all_to_all(payload, "ctx", split_axis=0, concat_axis=0, tiled=True)
    random_rows = jnp.take(received.reshape(slot_total, 2, BLOCK, local_width), slot_of, axis=0)
    random_rows = jnp.moveaxis(
        random_rows.reshape(seq_count, blocks_here, RMAX, 2, BLOCK, local_width), 3, 0
    )
    all_keys = jnp.concatenate([local_keys, random_rows], 3).reshape(
        2, seq_count, blocks_here, key_width * BLOCK, heads_here, HEAD_DIM
    )
    scores = (
        jnp.einsum(
            "sjqhd,sjkhd->sjhqk", query_view, all_keys[0], preferred_element_type=jnp.float32
        )
        * score_scale
    )
    live_slots = jnp.concatenate(
        [
            jnp.ones((seq_count, blocks_here, 3 + GLOB), jnp.bool_),
            slot_ids[None, None, :] < rand_count[:, :, None],
        ],
        2,
    )
    live_cols = jnp.repeat(live_slots, BLOCK, axis=2)[:, :, None, None, :]
    masked = jnp.where(live_cols, scores, -1e30)
    row_peak = jnp.max(masked, axis=-1, keepdims=True)
    weights = jnp.where(live_cols, jnp.exp(masked - row_peak), 0.0)
    row_total = jnp.sum(weights, axis=-1)
    weighted = jnp.einsum(
        "sjhqk,sjkhd->sjqhd",
        weights.astype(jnp.bfloat16),
        all_keys[1],
        preferred_element_type=jnp.float32,
    )
    attention = (
        (weighted / jnp.moveaxis(row_total, 2, 3)[..., None])
        .astype(jnp.bfloat16)
        .reshape(seq_count, seq_rows, local_width)
    )
    projected = jnp.einsum(
        "stf,fo->sto",
        lax.all_gather(attention, "head", axis=2, tiled=True),
        out_weight,
        preferred_element_type=jnp.float32,
    )
    return projected.astype(jnp.bfloat16)


NEAR = (1, 2, 3)
FAR = (4, 6, 5, 7)
EARLY, LATE = FAR[:2], FAR[2:]


def pack_near_kernel(me_ref, glob_hbm, rand_hbm, count_hbm, q_ref, k_ref, v_ref, *refs, ctx):
    near_ref, glob_ref, rand_ref, count_ref, id_sems, sems = refs
    seqs, rows, width = q_ref.shape
    me = me_ref[0]
    base = me - lax.rem(me, seqs)
    blocks_here = rows // BLOCK
    blocks = ctx * blocks_here
    tiles = ctx * rows // HEAD_DIM
    mask_rows = blocks_here * tiles
    ids = [
        pltpu.make_async_copy(src, dst, id_sems.at[i])
        for i, (src, dst) in enumerate(
            ((glob_hbm, glob_ref), (rand_hbm, rand_ref), (count_hbm, count_ref))
        )
    ]
    copies = [
        pltpu.make_async_copy(
            source.at[seq], near_ref.at[seq, pl.ds(start, rows), :], sems.at[3 * seq + i]
        )
        for seq in range(seqs)
        for i, (source, start) in enumerate(
            ((q_ref, 0), (k_ref, rows + mask_rows), (v_ref, 2 * rows + mask_rows))
        )
    ]
    for copy in ids + copies:
        copy.start()
    for copy in ids:
        copy.wait()
    tile = lax.broadcasted_iota(jnp.int32, (tiles, HEAD_DIM), 0)
    lane = lax.broadcasted_iota(jnp.int32, (tiles, HEAD_DIM), 1)
    for seq in range(seqs):
        holder = jnp.where(tile < seqs, base + tile, (base + seq) ^ tile)
        key_block = (holder * HEAD_DIM + lane) // BLOCK
        counts = []
        for j in range(blocks_here):
            block = me * blocks_here + j
            listed = [lax.rem(block + blocks - 1, blocks), block, lax.rem(block + 1, blocks)]
            listed += [glob_ref[g, seq] for g in range(GLOB)]
            listed += [
                jnp.where(r < count_ref[j, seq], rand_ref[seq, j, r], -1) for r in range(RMAX)
            ]
            counts.append(sum((key_block == one).astype(jnp.float32) for one in listed))
        counts = jnp.concatenate(counts, 0).astype(jnp.bfloat16)
        for h in range(width // HEAD_DIM):
            near_ref[seq, rows : rows + mask_rows, h * HEAD_DIM : (h + 1) * HEAD_DIM] = counts
    for copy in copies:
        copy.wait()


def stack_kernel(*refs):
    *parts, out_ref = refs
    for n, part in enumerate(parts):
        out_ref[n] = part[...]


def pieces_of(near_ref, early_ref, late_refs):
    pieces = [near_ref.at[n] for n in range(near_ref.shape[0])]
    return pieces + [early_ref.at[n] for n in range(early_ref.shape[0])] + list(late_refs)


def weigh_kernel(near_ref, early_ref, *refs, rows, tiles):
    *late_refs, weights_ref = refs
    pieces = pieces_of(near_ref, early_ref, late_refs)
    askers, _, width = near_ref.shape
    blocks_here = rows // BLOCK
    heads = width // HEAD_DIM
    scale = HEAD_DIM ** (-0.5) * 1.4426950408889634
    for n in range(askers):
        counts = near_ref[n, rows : rows + blocks_here * tiles, 0:HEAD_DIM].astype(jnp.float32)
        bias = jnp.where(counts > 0, jnp.log2(jnp.maximum(counts, 1.0)), -1e30)
        wide = jnp.concatenate(
            [
                jnp.concatenate(
                    [
                        jnp.broadcast_to(bias[j * tiles + i : j * tiles + i + 1, :], (BLOCK, HEAD_DIM))
                        for i in tuple(range(askers)) + FAR
                    ],
                    1,
                )
                for j in range(blocks_here)
            ],
            0,
        )
        for h in range(heads):
            cols = slice(h * HEAD_DIM, (h + 1) * HEAD_DIM)
            keys = [ref[ref.shape[0] - 2 * rows : ref.shape[0] - rows, cols] for ref in pieces]
            scores = lax.dot_general(
                near_ref[n, 0:rows, cols],
                jnp.concatenate(keys, 0),
                (((1,), (1,)), ((), ())),
                preferred_element_type=jnp.float32,
            )
            shifted = scores * scale + wide
            weights = jnp.exp2(shifted - jnp.max(shifted, axis=1, keepdims=True))
            weights_ref[n * heads + h] = weights.astype(jnp.bfloat16)


def sum_kernel(weights_ref, near_ref, early_ref, *refs, copies):
    *late_refs, out_ref = refs
    pieces = pieces_of(near_ref, early_ref, late_refs)
    count, rows, span = weights_ref.shape
    heads = near_ref.shape[2] // HEAD_DIM
    ones = jnp.ones((span, HEAD_DIM), jnp.bfloat16)
    for h in range(heads):
        cols = slice(h * HEAD_DIM, (h + 1) * HEAD_DIM)
        values = jnp.concatenate([ref[ref.shape[0] - rows :, cols] for ref in pieces], 0)
        both = jnp.concatenate([values, ones], 1)
        for n in range(count // heads):
            sums = jnp.dot(weights_ref[n * heads + h], both, preferred_element_type=jnp.float32)
            result = (sums[:, :HEAD_DIM] / sums[:, HEAD_DIM:]).astype(jnp.bfloat16)
            for copy in range(copies):
                out_ref[n * copies + copy, :, cols] = result


def project_kernel(group_ref, *refs, flip):
    *before, part_ref, weight_ref, out_ref = refs
    slots, rows, depth = part_ref.shape
    seqs = out_ref.shape[0]
    sides = slots // seqs
    core = lax.rem(group_ref[0], weight_ref.shape[0] // (depth * sides)) ^ flip
    weights = [
        weight_ref[pl.ds(pl.multiple_of((side * sides + core) * depth, depth), depth), :]
        for side in range(sides)
    ]
    for seq in range(seqs):
        total = before[0][seq] if before else 0.0
        for side in range(sides):
            total = total + jnp.dot(
                part_ref[seq * sides + side], weights[side], preferred_element_type=jnp.float32
            )
        out_ref[seq] = total.astype(out_ref.dtype)


def half_path(queries, keys, values, out_weight, global_ids, rand_ids, rand_count):
    seqs, rows, local_width = queries.shape
    ctx = lax.axis_size("ctx")
    groups = lax.axis_size("head")
    me = lax.axis_index("ctx").astype(jnp.int32).reshape(1)
    group = lax.axis_index("head").astype(jnp.int32).reshape(1)
    heads = local_width // HEAD_DIM
    tiles = ctx * rows // HEAD_DIM
    mask_rows = rows // BLOCK * tiles
    smem = pl.BlockSpec(memory_space=pltpu.SMEM)
    vmem = pl.BlockSpec(memory_space=pltpu.VMEM)
    anywhere = pl.BlockSpec(memory_space=pl.ANY)
    all_room = pltpu.CompilerParams(vmem_limit_bytes=60 << 20)
    room = pltpu.CompilerParams(vmem_limit_bytes=8 << 20)
    high = 3 * rows + mask_rows
    def far_piece(flip):
        seq = (me[0] ^ flip) % seqs
        take = lambda block: lax.dynamic_slice_in_dim(block, seq, 1, 0)[0]
        return jnp.concatenate([take(keys), take(values)], 0)

    sent = [far_piece(flip) for flip in FAR]
    packed = pl.pallas_call(
        functools.partial(pack_near_kernel, ctx=ctx),
        in_specs=[smem] + [anywhere] * 6,
        out_specs=vmem,
        out_shape=jax.ShapeDtypeStruct((seqs, high, local_width), jnp.bfloat16),
        scratch_shapes=[
            pltpu.SMEM((GLOB, seqs), jnp.int32),
            pltpu.SMEM((seqs, rows // BLOCK, RMAX), jnp.int32),
            pltpu.SMEM((rows // BLOCK, seqs), jnp.int32),
            pltpu.SemaphoreType.DMA((3,)),
            pltpu.SemaphoreType.DMA((3 * seqs,)),
        ],
        compiler_params=all_room,
        name="pack_near",
    )(me, global_ids.T, rand_ids, rand_count.T, queries, keys, values)
    got = {
        flip: lax.ppermute(part, "ctx", [(i, i ^ flip) for i in range(ctx)])
        for flip, part in zip(FAR, sent)
    }
    halves = [[half * seqs + c for c in range(seqs)] for half in range(ctx // seqs)]
    near = lax.all_to_all(packed, "ctx", split_axis=0, concat_axis=0, tiled=True, axis_index_groups=halves)
    early = pl.pallas_call(
        stack_kernel,
        in_specs=[vmem] * len(EARLY),
        out_specs=vmem,
        out_shape=jax.ShapeDtypeStruct((len(EARLY), 2 * rows, local_width), jnp.bfloat16),
        compiler_params=room,
        cost_estimate=pl.CostEstimate(flops=11 * 10**9, bytes_accessed=0, transcendentals=0),
        name="stack",
    )(*[got[flip] for flip in EARLY])
    late = [got[flip] for flip in LATE]
    pairs = heads * seqs * rows * ctx * rows
    cost = pl.CostEstimate(
        flops=2 * pairs * HEAD_DIM, bytes_accessed=2 * pairs, transcendentals=pairs
    )
    weights = pl.pallas_call(
        functools.partial(weigh_kernel, rows=rows, tiles=tiles),
        in_specs=[vmem] * (2 + len(late)),
        out_specs=vmem,
        out_shape=jax.ShapeDtypeStruct((seqs * heads, rows, ctx * rows), jnp.bfloat16),
        compiler_params=room,
        cost_estimate=cost,
        name="weigh",
    )(near, early, *late)
    sides = 2
    attention = pl.pallas_call(
        functools.partial(sum_kernel, copies=sides),
        in_specs=[vmem] * (3 + len(late)),
        out_specs=vmem,
        out_shape=jax.ShapeDtypeStruct((seqs * sides, rows, local_width), jnp.bfloat16),
        compiler_params=room,
        cost_estimate=cost,
        name="sum",
    )(weights, near, early, *late)
    cores = groups // sides
    home = lax.all_to_all(
        attention,
        ("ctx", "head"),
        split_axis=0,
        concat_axis=0,
        tiled=True,
        axis_index_groups=[
            [(half * seqs + c) * groups + side * cores + core for c in range(seqs) for side in range(sides)]
            for half in range(ctx // seqs)
            for core in range(cores)
        ],
    )
    beside = lax.ppermute(home, "head", [(i, i ^ 1) for i in range(groups)])
    width = out_weight.shape[1]

    def project(flip, dtype, *parts):
        return pl.pallas_call(
            functools.partial(project_kernel, flip=flip),
            in_specs=[smem] + [vmem] * (len(parts) + 1),
            out_specs=vmem,
            out_shape=jax.ShapeDtypeStruct((seqs, rows, width), dtype),
            compiler_params=room,
            cost_estimate=pl.CostEstimate(
                flops=seqs * rows * width * out_weight.shape[0],
                bytes_accessed=4 * seqs * rows * width,
                transcendentals=0,
            ),
            name="project",
        )(group, *parts, out_weight)

    return project(1, jnp.bfloat16, project(0, jnp.float32, home), beside)


def on_device(queries, keys, values, out_weight, global_ids, rand_ids, rand_count):
    seqs, rows, local_width = queries.shape
    ctx, groups = lax.axis_size("ctx"), lax.axis_size("head")
    fits = ctx == 2 * seqs == 8 and groups == 4 and rows == HEAD_DIM == 2 * BLOCK
    path = half_path if fits else general_path
    return path(queries, keys, values, out_weight, global_ids, rand_ids, rand_count)


def solution(mesh):
    placed = (
        P(None, "ctx", "head"),
        P(None, "ctx", "head"),
        P(None, "ctx", "head"),
        P(None, "head"),
        P(),
        P(None, "ctx", None),
        P(None, "ctx"),
    )
    return jax.shard_map(
        on_device, mesh=mesh, in_specs=placed, out_specs=P(None, "ctx", "head"), check_vma=False
    )
```

```python
import functools

import jax
import jax.numpy as jnp
from jax import lax
from jax.experimental import pallas as pl
from jax.experimental.pallas import tpu as pltpu
from jax.sharding import PartitionSpec as P

HEAD_DIM = 128
BLOCK = 64
GLOB = 2
RMAX = 4


def with_halo(cells, sides, width):
    for axis, dim in sides:
        count = lax.axis_size(axis)
        head = lax.slice_in_dim(cells, 0, width, axis=dim)
        tail = lax.slice_in_dim(cells, cells.shape[dim] - width, cells.shape[dim], axis=dim)
        cells = jnp.concatenate(
            [
                lax.ppermute(tail, axis, [(i, (i + 1) % count) for i in range(count)]),
                cells,
                lax.ppermute(head, axis, [((i + 1) % count, i) for i in range(count)]),
            ],
            axis=dim,
        )
    return cells


def slot_table(slot_of, live_flat, slot_total):
    return (
        (slot_of[:, None] == jnp.arange(slot_total, dtype=jnp.int32)[None, :]) & live_flat[:, None]
    ).astype(jnp.int32)


def general_path(queries, keys, values, out_weight, global_ids, rand_ids, rand_count):
    seq_count, seq_rows, local_width = queries.shape
    blocks_here = seq_rows // BLOCK
    heads_here = local_width // HEAD_DIM
    cycle_size = lax.axis_size("ctx")
    my_index = lax.axis_index("ctx")
    request_count = seq_count * blocks_here * RMAX
    capacity = (request_count + cycle_size - 1) // cycle_size
    slot_total = cycle_size * capacity
    key_width = 3 + GLOB + RMAX
    score_scale = HEAD_DIM ** (-0.5)
    token_pairs = jnp.stack([keys, values], 0)
    block_pairs = jnp.stack(
        [
            keys.reshape(seq_count, blocks_here, BLOCK, local_width),
            values.reshape(seq_count, blocks_here, BLOCK, local_width),
        ],
        2,
    ).reshape(seq_count * blocks_here, 2, BLOCK, local_width)
    extended = with_halo(token_pairs, (("ctx", 2),), BLOCK)
    own_blocks = token_pairs.reshape(2, seq_count, blocks_here, BLOCK, local_width)
    shared_owner = global_ids // blocks_here
    shared_local = global_ids % blocks_here
    picker = (
        (shared_local[:, :, None] == jnp.arange(blocks_here, dtype=jnp.int32)[None, None, :])
        & (shared_owner == my_index)[:, :, None]
    ).astype(jnp.bfloat16)
    contribution = jnp.einsum(
        "sgj,xsjtf->xsgtf", picker, own_blocks, preferred_element_type=jnp.float32
    )
    shared_rows = lax.psum(contribution, "ctx").astype(jnp.bfloat16)
    slot_ids = jnp.arange(RMAX, dtype=jnp.int32)
    live_flat = (slot_ids[None, None, :] < rand_count[:, :, None]).reshape(-1)
    owners = (rand_ids // blocks_here).reshape(-1)
    seq_of = jnp.arange(seq_count, dtype=jnp.int32)[:, None, None]
    block_codes = (seq_of * blocks_here + rand_ids % blocks_here).reshape(-1)
    hit_owner = (
        (owners[:, None] == jnp.arange(cycle_size, dtype=jnp.int32)[None, :]) & live_flat[:, None]
    ).astype(jnp.int32)
    rank_within = jnp.sum((jnp.cumsum(hit_owner, axis=0) - hit_owner) * hit_owner, axis=1)
    slot_of = jnp.where(live_flat, owners * capacity + rank_within, 0)
    slot_hits = slot_table(slot_of, live_flat, slot_total)
    requests_out = (jnp.sum(slot_hits * (block_codes[:, None] + 1), axis=0) - 1).reshape(
        cycle_size, capacity
    )
    wanted_here = lax.all_to_all(requests_out, "ctx", split_axis=0, concat_axis=0, tiled=True)
    beside_all = extended.reshape(2, seq_count, blocks_here + 2, BLOCK, local_width)
    window_keys = jnp.stack(
        [beside_all[:, :, offset : offset + blocks_here] for offset in range(3)], 3
    )
    shared_wide = jnp.broadcast_to(
        shared_rows[:, :, None], (2, seq_count, blocks_here, GLOB, BLOCK, local_width)
    )
    local_keys = jnp.concatenate([window_keys, shared_wide], 3)
    query_view = queries.reshape(seq_count, blocks_here, BLOCK, heads_here, HEAD_DIM)
    payload = jnp.take(block_pairs, jnp.maximum(wanted_here, 0).reshape(-1), axis=0).reshape(
        cycle_size, capacity, 2, BLOCK, local_width
    )
    received = lax.all_to_all(payload, "ctx", split_axis=0, concat_axis=0, tiled=True)
    random_rows = jnp.take(received.reshape(slot_total, 2, BLOCK, local_width), slot_of, axis=0)
    random_rows = jnp.moveaxis(
        random_rows.reshape(seq_count, blocks_here, RMAX, 2, BLOCK, local_width), 3, 0
    )
    all_keys = jnp.concatenate([local_keys, random_rows], 3).reshape(
        2, seq_count, blocks_here, key_width * BLOCK, heads_here, HEAD_DIM
    )
    scores = (
        jnp.einsum(
            "sjqhd,sjkhd->sjhqk", query_view, all_keys[0], preferred_element_type=jnp.float32
        )
        * score_scale
    )
    live_slots = jnp.concatenate(
        [
            jnp.ones((seq_count, blocks_here, 3 + GLOB), jnp.bool_),
            slot_ids[None, None, :] < rand_count[:, :, None],
        ],
        2,
    )
    live_cols = jnp.repeat(live_slots, BLOCK, axis=2)[:, :, None, None, :]
    masked = jnp.where(live_cols, scores, -1e30)
    row_peak = jnp.max(masked, axis=-1, keepdims=True)
    weights = jnp.where(live_cols, jnp.exp(masked - row_peak), 0.0)
    row_total = jnp.sum(weights, axis=-1)
    weighted = jnp.einsum(
        "sjhqk,sjkhd->sjqhd",
        weights.astype(jnp.bfloat16),
        all_keys[1],
        preferred_element_type=jnp.float32,
    )
    attention = (
        (weighted / jnp.moveaxis(row_total, 2, 3)[..., None])
        .astype(jnp.bfloat16)
        .reshape(seq_count, seq_rows, local_width)
    )
    projected = jnp.einsum(
        "stf,fo->sto",
        lax.all_gather(attention, "head", axis=2, tiled=True),
        out_weight,
        preferred_element_type=jnp.float32,
    )
    return projected.astype(jnp.bfloat16)


NEAR = (1, 2, 3)
FAR = (6, 5, 4, 7)
EARLY, LATE = FAR, ()


def count_kernel(me_ref, glob_ref, rand_ref, count_ref, *outs, ctx):
    seqs = rand_ref.shape[0]
    blocks_here = rand_ref.shape[1]
    mask_rows = outs[0].shape[0]
    tiles = mask_rows // blocks_here
    blocks = ctx * blocks_here
    me = me_ref[0]
    base = me - lax.rem(me, seqs)
    tile = lax.broadcasted_iota(jnp.int32, (tiles, HEAD_DIM), 0)
    lane = lax.broadcasted_iota(jnp.int32, (tiles, HEAD_DIM), 1)
    for flip, out in enumerate(outs):
        asker = me ^ flip
        seq = lax.rem(asker, seqs)
        holder = jnp.where(tile < seqs, base + tile, asker ^ tile)
        key_block = (holder * HEAD_DIM + lane) // BLOCK
        counts = []
        for j in range(blocks_here):
            block = me * blocks_here + j
            listed = [lax.rem(block + blocks - 1, blocks), block, lax.rem(block + 1, blocks)]
            listed += [glob_ref[g, seq] for g in range(GLOB)]
            listed += [
                jnp.where(r < count_ref[j, seq], rand_ref[seq, j, r], -1) for r in range(RMAX)
            ]
            counts.append(sum((key_block == one).astype(jnp.float32) for one in listed))
        out[...] = jnp.concatenate(counts, 0).astype(jnp.bfloat16)


def stack_kernel(*refs):
    *parts, out_ref = refs
    for n, part in enumerate(parts):
        out_ref[n] = part[...]


def pieces_of(near_ref, early_ref, late_refs):
    pieces = [near_ref.at[n] for n in range(near_ref.shape[0])]
    return pieces + [early_ref.at[n] for n in range(early_ref.shape[0])] + list(late_refs)


def weigh_kernel(me_ref, near_ref, early_ref, *refs, rows, tiles, late):
    *refs, weights_ref = refs
    late_refs, counts_refs = refs[:late], refs[late:]
    pieces = pieces_of(near_ref, early_ref, late_refs)
    askers, _, width = near_ref.shape
    spot = lax.rem(me_ref[0], askers)
    blocks_here = rows // BLOCK
    heads = width // HEAD_DIM
    scale = HEAD_DIM ** (-0.5) * 1.4426950408889634
    for n in range(askers):
        counts = counts_refs[n][...].astype(jnp.float32)
        bias = jnp.where(counts > 0, jnp.log2(jnp.maximum(counts, 1.0)), -1e30)
        wide = jnp.concatenate(
            [
                jnp.concatenate(
                    [
                        jnp.broadcast_to(bias[j * tiles + i : j * tiles + i + 1, :], (BLOCK, HEAD_DIM))
                        for i in tuple(range(askers)) + FAR
                    ],
                    1,
                )
                for j in range(blocks_here)
            ],
            0,
        )
        for h in range(heads):
            cols = slice(h * HEAD_DIM, (h + 1) * HEAD_DIM)
            keys = [ref[ref.shape[0] - 2 * rows : ref.shape[0] - rows, cols] for ref in pieces]
            scores = lax.dot_general(
                near_ref[spot ^ n, 0:rows, cols],
                jnp.concatenate(keys, 0),
                (((1,), (1,)), ((), ())),
                preferred_element_type=jnp.float32,
            )
            shifted = scores * scale + wide
            weights = jnp.exp2(shifted - jnp.max(shifted, axis=1, keepdims=True))
            weights_ref[n * heads + h] = weights.astype(jnp.bfloat16)


def sum_kernel(me_ref, weights_ref, near_ref, early_ref, *refs, copies):
    *late_refs, out_ref = refs
    pieces = pieces_of(near_ref, early_ref, late_refs)
    count, rows, span = weights_ref.shape
    spot = lax.rem(me_ref[0], near_ref.shape[0])
    heads = near_ref.shape[2] // HEAD_DIM
    ones = jnp.ones((span, HEAD_DIM), jnp.bfloat16)
    for h in range(heads):
        cols = slice(h * HEAD_DIM, (h + 1) * HEAD_DIM)
        values = jnp.concatenate([ref[ref.shape[0] - rows :, cols] for ref in pieces], 0)
        both = jnp.concatenate([values, ones], 1)
        for n in range(count // heads):
            sums = jnp.dot(weights_ref[n * heads + h], both, preferred_element_type=jnp.float32)
            result = (sums[:, :HEAD_DIM] / sums[:, HEAD_DIM:]).astype(jnp.bfloat16)
            for copy in range(copies):
                out_ref[(spot ^ n) * copies + copy, :, cols] = result


def project_kernel(group_ref, *refs, flip):
    *before, part_ref, weight_ref, out_ref = refs
    slots, rows, depth = part_ref.shape
    seqs = out_ref.shape[0]
    sides = slots // seqs
    cores = weight_ref.shape[0] // (depth * sides)
    core = lax.rem(group_ref[0], cores) ^ flip
    weights = [
        weight_ref[pl.ds(pl.multiple_of((side * cores + core) * depth, depth), depth), :]
        for side in range(sides)
    ]
    for seq in range(seqs):
        total = before[0][seq] if before else 0.0
        for side in range(sides):
            total = total + jnp.dot(
                part_ref[seq * sides + side], weights[side], preferred_element_type=jnp.float32
            )
        out_ref[seq] = total.astype(out_ref.dtype)


def finish_kernel(group_ref, before_ref, part_ref, weight_ref, *refs, flip, first):
    *_, out_ref, buffer, sems = refs
    slots, rows, depth = part_ref.shape
    sides = slots // buffer.shape[0]
    cores = weight_ref.shape[0] // (depth * sides)
    core = lax.rem(group_ref[0], cores) ^ flip
    weights = [
        weight_ref[pl.ds(pl.multiple_of((side * cores + core) * depth, depth), depth), :]
        for side in range(sides)
    ]
    copies = []
    for n in range(buffer.shape[0]):
        total = before_ref[first + n]
        for side in range(sides):
            total = total + jnp.dot(
                part_ref[n * sides + side], weights[side], preferred_element_type=jnp.float32
            )
        buffer[n] = total.astype(buffer.dtype)
        copies.append(pltpu.make_async_copy(buffer.at[n], out_ref.at[first + n], sems.at[n]))
        copies[-1].start()
    for copy in copies:
        copy.wait()


def half_path(queries, keys, values, out_weight, global_ids, rand_ids, rand_count):
    seqs, rows, local_width = queries.shape
    ctx = lax.axis_size("ctx")
    groups = lax.axis_size("head")
    me = lax.axis_index("ctx").astype(jnp.int32).reshape(1)
    group = lax.axis_index("head").astype(jnp.int32).reshape(1)
    heads = local_width // HEAD_DIM
    tiles = ctx * rows // HEAD_DIM
    mask_rows = rows // BLOCK * tiles
    smem = pl.BlockSpec(memory_space=pltpu.SMEM)
    vmem = pl.BlockSpec(memory_space=pltpu.VMEM)
    anywhere = pl.BlockSpec(memory_space=pl.ANY)
    room = pltpu.CompilerParams(vmem_limit_bytes=8 << 20)
    def far_piece(flip):
        seq = (me[0] ^ flip) % seqs
        take = lambda block: lax.dynamic_slice_in_dim(block, seq, 1, 0)[0]
        return jnp.concatenate([take(keys), take(values)], 0)

    sent = [far_piece(flip) for flip in FAR]
    own, *asked = pl.pallas_call(
        functools.partial(count_kernel, ctx=ctx),
        in_specs=[smem] * 4,
        out_specs=[vmem] * seqs,
        out_shape=[jax.ShapeDtypeStruct((mask_rows, HEAD_DIM), jnp.bfloat16)] * seqs,
        compiler_params=room,
        name="count",
    )(me, global_ids.T, rand_ids, rand_count.T)
    packed = jnp.concatenate([queries, keys, values], 1)
    got = {
        flip: lax.ppermute(part, "ctx", [(i, i ^ flip) for i in range(ctx)])
        for flip, part in zip(FAR, sent)
    }
    halves = [[half * seqs + c for c in range(seqs)] for half in range(ctx // seqs)]
    near = lax.all_to_all(packed, "ctx", split_axis=0, concat_axis=0, tiled=True, axis_index_groups=halves)
    counts = [own] + [
        lax.ppermute(part, "ctx", [(i, i ^ (n + 1)) for i in range(ctx)]) for n, part in enumerate(asked)
    ]
    early = pl.pallas_call(
        stack_kernel,
        in_specs=[vmem] * len(EARLY),
        out_specs=vmem,
        out_shape=jax.ShapeDtypeStruct((len(EARLY), 2 * rows, local_width), jnp.bfloat16),
        compiler_params=room,
        cost_estimate=pl.CostEstimate(flops=9 * 10**9, bytes_accessed=0, transcendentals=0),
        name="stack",
    )(*[got[flip] for flip in EARLY])
    late = [got[flip] for flip in LATE]
    pairs = heads * seqs * rows * ctx * rows
    cost = pl.CostEstimate(
        flops=2 * pairs * HEAD_DIM, bytes_accessed=2 * pairs, transcendentals=pairs
    )
    weights = pl.pallas_call(
        functools.partial(weigh_kernel, rows=rows, tiles=tiles, late=len(late)),
        in_specs=[smem] + [vmem] * (2 + len(late) + seqs),
        out_specs=vmem,
        out_shape=jax.ShapeDtypeStruct((seqs * heads, rows, ctx * rows), jnp.bfloat16),
        compiler_params=room,
        cost_estimate=cost,
        name="weigh",
    )(me, near, early, *late, *counts)
    sides = 2
    attention = pl.pallas_call(
        functools.partial(sum_kernel, copies=sides),
        in_specs=[smem] + [vmem] * (3 + len(late)),
        out_specs=vmem,
        out_shape=jax.ShapeDtypeStruct((seqs * sides, rows, local_width), jnp.bfloat16),
        compiler_params=room,
        cost_estimate=cost,
        name="sum",
    )(me, weights, near, early, *late)
    cores = groups // sides
    home = lax.all_to_all(
        attention,
        ("ctx", "head"),
        split_axis=0,
        concat_axis=0,
        tiled=True,
        axis_index_groups=[
            [(half * seqs + c) * groups + side * cores + core for c in range(seqs) for side in range(sides)]
            for half in range(ctx // seqs)
            for core in range(cores)
        ],
    )
    beside = lax.ppermute(home, "head", [(i, i ^ 1) for i in range(groups)])
    width = out_weight.shape[1]

    def project(flip, dtype, *parts):
        return pl.pallas_call(
            functools.partial(project_kernel, flip=flip),
            in_specs=[smem] + [vmem] * (len(parts) + 1),
            out_specs=vmem,
            out_shape=jax.ShapeDtypeStruct((seqs, rows, width), dtype),
            compiler_params=room,
            cost_estimate=pl.CostEstimate(
                flops=seqs * rows * width * out_weight.shape[0],
                bytes_accessed=4 * seqs * rows * width,
                transcendentals=0,
            ),
            name="project",
        )(group, *parts, out_weight)

    return pl.pallas_call(
        functools.partial(finish_kernel, flip=1, first=0),
        in_specs=[smem] + [vmem] * 3,
        out_specs=anywhere,
        out_shape=jax.ShapeDtypeStruct((seqs, rows, width), jnp.bfloat16),
        scratch_shapes=[
            pltpu.VMEM((seqs, rows, width), jnp.bfloat16),
            pltpu.SemaphoreType.DMA((seqs,)),
        ],
        compiler_params=room,
        name="finish",
    )(group, project(0, jnp.float32, home), beside, out_weight)


def on_device(queries, keys, values, out_weight, global_ids, rand_ids, rand_count):
    seqs, rows, local_width = queries.shape
    ctx, groups = lax.axis_size("ctx"), lax.axis_size("head")
    fits = ctx == 2 * seqs == 8 and groups == 4 and rows == HEAD_DIM == 2 * BLOCK
    path = half_path if fits else general_path
    return path(queries, keys, values, out_weight, global_ids, rand_ids, rand_count)


def solution(mesh):
    placed = (
        P(None, "ctx", "head"),
        P(None, "ctx", "head"),
        P(None, "ctx", "head"),
        P(None, "head"),
        P(),
        P(None, "ctx", None),
        P(None, "ctx"),
    )
    return jax.shard_map(
        on_device, mesh=mesh, in_specs=placed, out_specs=P(None, "ctx", "head"), check_vma=False
    )
```

```python
import functools

import jax
import jax.numpy as jnp
from jax import lax
from jax.experimental import pallas as pl
from jax.experimental.pallas import tpu as pltpu
from jax.sharding import PartitionSpec as P

HEAD_DIM = 128
BLOCK = 64
GLOB = 2
RMAX = 4


def with_halo(cells, sides, width):
    for axis, dim in sides:
        count = lax.axis_size(axis)
        head = lax.slice_in_dim(cells, 0, width, axis=dim)
        tail = lax.slice_in_dim(cells, cells.shape[dim] - width, cells.shape[dim], axis=dim)
        cells = jnp.concatenate(
            [
                lax.ppermute(tail, axis, [(i, (i + 1) % count) for i in range(count)]),
                cells,
                lax.ppermute(head, axis, [((i + 1) % count, i) for i in range(count)]),
            ],
            axis=dim,
        )
    return cells


def slot_table(slot_of, live_flat, slot_total):
    return (
        (slot_of[:, None] == jnp.arange(slot_total, dtype=jnp.int32)[None, :]) & live_flat[:, None]
    ).astype(jnp.int32)


def general_path(queries, keys, values, out_weight, global_ids, rand_ids, rand_count):
    seq_count, seq_rows, local_width = queries.shape
    blocks_here = seq_rows // BLOCK
    heads_here = local_width // HEAD_DIM
    cycle_size = lax.axis_size("ctx")
    my_index = lax.axis_index("ctx")
    request_count = seq_count * blocks_here * RMAX
    capacity = (request_count + cycle_size - 1) // cycle_size
    slot_total = cycle_size * capacity
    key_width = 3 + GLOB + RMAX
    score_scale = HEAD_DIM ** (-0.5)
    token_pairs = jnp.stack([keys, values], 0)
    block_pairs = jnp.stack(
        [
            keys.reshape(seq_count, blocks_here, BLOCK, local_width),
            values.reshape(seq_count, blocks_here, BLOCK, local_width),
        ],
        2,
    ).reshape(seq_count * blocks_here, 2, BLOCK, local_width)
    extended = with_halo(token_pairs, (("ctx", 2),), BLOCK)
    own_blocks = token_pairs.reshape(2, seq_count, blocks_here, BLOCK, local_width)
    shared_owner = global_ids // blocks_here
    shared_local = global_ids % blocks_here
    picker = (
        (shared_local[:, :, None] == jnp.arange(blocks_here, dtype=jnp.int32)[None, None, :])
        & (shared_owner == my_index)[:, :, None]
    ).astype(jnp.bfloat16)
    contribution = jnp.einsum(
        "sgj,xsjtf->xsgtf", picker, own_blocks, preferred_element_type=jnp.float32
    )
    shared_rows = lax.psum(contribution, "ctx").astype(jnp.bfloat16)
    slot_ids = jnp.arange(RMAX, dtype=jnp.int32)
    live_flat = (slot_ids[None, None, :] < rand_count[:, :, None]).reshape(-1)
    owners = (rand_ids // blocks_here).reshape(-1)
    seq_of = jnp.arange(seq_count, dtype=jnp.int32)[:, None, None]
    block_codes = (seq_of * blocks_here + rand_ids % blocks_here).reshape(-1)
    hit_owner = (
        (owners[:, None] == jnp.arange(cycle_size, dtype=jnp.int32)[None, :]) & live_flat[:, None]
    ).astype(jnp.int32)
    rank_within = jnp.sum((jnp.cumsum(hit_owner, axis=0) - hit_owner) * hit_owner, axis=1)
    slot_of = jnp.where(live_flat, owners * capacity + rank_within, 0)
    slot_hits = slot_table(slot_of, live_flat, slot_total)
    requests_out = (jnp.sum(slot_hits * (block_codes[:, None] + 1), axis=0) - 1).reshape(
        cycle_size, capacity
    )
    wanted_here = lax.all_to_all(requests_out, "ctx", split_axis=0, concat_axis=0, tiled=True)
    beside_all = extended.reshape(2, seq_count, blocks_here + 2, BLOCK, local_width)
    window_keys = jnp.stack(
        [beside_all[:, :, offset : offset + blocks_here] for offset in range(3)], 3
    )
    shared_wide = jnp.broadcast_to(
        shared_rows[:, :, None], (2, seq_count, blocks_here, GLOB, BLOCK, local_width)
    )
    local_keys = jnp.concatenate([window_keys, shared_wide], 3)
    query_view = queries.reshape(seq_count, blocks_here, BLOCK, heads_here, HEAD_DIM)
    payload = jnp.take(block_pairs, jnp.maximum(wanted_here, 0).reshape(-1), axis=0).reshape(
        cycle_size, capacity, 2, BLOCK, local_width
    )
    received = lax.all_to_all(payload, "ctx", split_axis=0, concat_axis=0, tiled=True)
    random_rows = jnp.take(received.reshape(slot_total, 2, BLOCK, local_width), slot_of, axis=0)
    random_rows = jnp.moveaxis(
        random_rows.reshape(seq_count, blocks_here, RMAX, 2, BLOCK, local_width), 3, 0
    )
    all_keys = jnp.concatenate([local_keys, random_rows], 3).reshape(
        2, seq_count, blocks_here, key_width * BLOCK, heads_here, HEAD_DIM
    )
    scores = (
        jnp.einsum(
            "sjqhd,sjkhd->sjhqk", query_view, all_keys[0], preferred_element_type=jnp.float32
        )
        * score_scale
    )
    live_slots = jnp.concatenate(
        [
            jnp.ones((seq_count, blocks_here, 3 + GLOB), jnp.bool_),
            slot_ids[None, None, :] < rand_count[:, :, None],
        ],
        2,
    )
    live_cols = jnp.repeat(live_slots, BLOCK, axis=2)[:, :, None, None, :]
    masked = jnp.where(live_cols, scores, -1e30)
    row_peak = jnp.max(masked, axis=-1, keepdims=True)
    weights = jnp.where(live_cols, jnp.exp(masked - row_peak), 0.0)
    row_total = jnp.sum(weights, axis=-1)
    weighted = jnp.einsum(
        "sjhqk,sjkhd->sjqhd",
        weights.astype(jnp.bfloat16),
        all_keys[1],
        preferred_element_type=jnp.float32,
    )
    attention = (
        (weighted / jnp.moveaxis(row_total, 2, 3)[..., None])
        .astype(jnp.bfloat16)
        .reshape(seq_count, seq_rows, local_width)
    )
    projected = jnp.einsum(
        "stf,fo->sto",
        lax.all_gather(attention, "head", axis=2, tiled=True),
        out_weight,
        preferred_element_type=jnp.float32,
    )
    return projected.astype(jnp.bfloat16)


NEAR = (1, 2, 3)
FAR = (4, 5, 6, 7)
EARLY, LATE = FAR, ()


def count_kernel(me_ref, glob_ref, rand_ref, count_ref, *outs, ctx):
    seqs = rand_ref.shape[0]
    blocks_here = rand_ref.shape[1]
    mask_rows = outs[0].shape[0]
    tiles = mask_rows // blocks_here
    blocks = ctx * blocks_here
    me = me_ref[0]
    base = me - lax.rem(me, seqs)
    tile = lax.broadcasted_iota(jnp.int32, (tiles, HEAD_DIM), 0)
    lane = lax.broadcasted_iota(jnp.int32, (tiles, HEAD_DIM), 1)
    for flip, out in enumerate(outs):
        asker = me ^ flip
        seq = lax.rem(asker, seqs)
        holder = jnp.where(tile < seqs, base + tile, asker ^ tile)
        key_block = (holder * HEAD_DIM + lane) // BLOCK
        counts = []
        for j in range(blocks_here):
            block = me * blocks_here + j
            listed = [lax.rem(block + blocks - 1, blocks), block, lax.rem(block + 1, blocks)]
            listed += [glob_ref[g, seq] for g in range(GLOB)]
            listed += [
                jnp.where(r < count_ref[j, seq], rand_ref[seq, j, r], -1) for r in range(RMAX)
            ]
            counts.append(sum((key_block == one).astype(jnp.float32) for one in listed))
        out[...] = jnp.concatenate(counts, 0).astype(jnp.bfloat16)


def stack_kernel(*refs):
    *parts, out_ref = refs
    for n, part in enumerate(parts):
        out_ref[n] = part[...]


def pieces_of(near_ref, early_ref, late_refs):
    pieces = [near_ref.at[n] for n in range(near_ref.shape[0])]
    return pieces + [early_ref.at[n] for n in range(early_ref.shape[0])] + list(late_refs)


def weigh_kernel(me_ref, near_ref, early_ref, *refs, rows, tiles, late):
    *refs, weights_ref = refs
    late_refs, counts_refs = refs[:late], refs[late:]
    pieces = pieces_of(near_ref, early_ref, late_refs)
    askers, _, width = near_ref.shape
    spot = lax.rem(me_ref[0], askers)
    blocks_here = rows // BLOCK
    heads = width // HEAD_DIM
    scale = HEAD_DIM ** (-0.5) * 1.4426950408889634
    biases = []
    for n in range(askers):
        counts = counts_refs[n][...].astype(jnp.float32)
        biases.append(jnp.where(counts > 0, jnp.log2(jnp.maximum(counts, 1.0)), -1e30))
    for h in range(heads):
        cols = slice(h * HEAD_DIM, (h + 1) * HEAD_DIM)
        keys = [ref[ref.shape[0] - 2 * rows : ref.shape[0] - rows, cols] for ref in pieces]
        scores = lax.dot_general(
            jnp.concatenate([near_ref[spot ^ n, 0:rows, cols] for n in range(askers)], 0),
            jnp.concatenate(keys, 0),
            (((1,), (1,)), ((), ())),
            preferred_element_type=jnp.float32,
        )
        for n in range(askers):
            for j in range(blocks_here):
                at = n * rows + j * BLOCK
                wide = jnp.concatenate(
                    [biases[n][j * tiles + i : j * tiles + i + 1, :] for i in tuple(range(askers)) + FAR], 1
                )
                shifted = scores[at : at + BLOCK] * scale + wide
                weights = jnp.exp2(shifted - jnp.max(shifted, axis=1, keepdims=True))
                weights_ref[n * heads + h, j * BLOCK : (j + 1) * BLOCK, :] = weights.astype(jnp.bfloat16)


def sum_kernel(me_ref, weights_ref, near_ref, early_ref, *refs, copies):
    *late_refs, out_ref = refs
    pieces = pieces_of(near_ref, early_ref, late_refs)
    count, rows, span = weights_ref.shape
    spot = lax.rem(me_ref[0], near_ref.shape[0])
    heads = near_ref.shape[2] // HEAD_DIM
    ones = jnp.ones((span, HEAD_DIM), jnp.bfloat16)
    for h in range(heads):
        cols = slice(h * HEAD_DIM, (h + 1) * HEAD_DIM)
        values = jnp.concatenate([ref[ref.shape[0] - rows :, cols] for ref in pieces], 0)
        both = jnp.concatenate([values, ones], 1)
        for n in range(count // heads):
            sums = jnp.dot(weights_ref[n * heads + h], both, preferred_element_type=jnp.float32)
            result = (sums[:, :HEAD_DIM] / sums[:, HEAD_DIM:]).astype(jnp.bfloat16)
            for copy in range(copies):
                out_ref[(spot ^ n) * copies + copy, :, cols] = result


def project_kernel(group_ref, *refs, flip):
    *before, part_ref, weight_ref, out_ref = refs
    slots, rows, depth = part_ref.shape
    seqs = out_ref.shape[0]
    sides = slots // seqs
    cores = weight_ref.shape[0] // (depth * sides)
    core = lax.rem(group_ref[0], cores) ^ flip
    weights = [
        weight_ref[pl.ds(pl.multiple_of((side * cores + core) * depth, depth), depth), :]
        for side in range(sides)
    ]
    for seq in range(seqs):
        total = before[0][seq] if before else 0.0
        for side in range(sides):
            total = total + jnp.dot(
                part_ref[seq * sides + side], weights[side], preferred_element_type=jnp.float32
            )
        out_ref[seq] = total.astype(out_ref.dtype)


def finish_kernel(group_ref, before_ref, part_ref, weight_ref, *refs, flip, first):
    *_, out_ref, buffer, sems = refs
    slots, rows, depth = part_ref.shape
    sides = slots // buffer.shape[0]
    cores = weight_ref.shape[0] // (depth * sides)
    core = lax.rem(group_ref[0], cores) ^ flip
    weights = [
        weight_ref[pl.ds(pl.multiple_of((side * cores + core) * depth, depth), depth), :]
        for side in range(sides)
    ]
    copies = []
    for n in range(buffer.shape[0]):
        total = before_ref[first + n]
        for side in range(sides):
            total = total + jnp.dot(
                part_ref[n * sides + side], weights[side], preferred_element_type=jnp.float32
            )
        buffer[n] = total.astype(buffer.dtype)
        copies.append(pltpu.make_async_copy(buffer.at[n], out_ref.at[first + n], sems.at[n]))
        copies[-1].start()
    for copy in copies:
        copy.wait()


def half_path(queries, keys, values, out_weight, global_ids, rand_ids, rand_count):
    seqs, rows, local_width = queries.shape
    ctx = lax.axis_size("ctx")
    groups = lax.axis_size("head")
    me = lax.axis_index("ctx").astype(jnp.int32).reshape(1)
    group = lax.axis_index("head").astype(jnp.int32).reshape(1)
    heads = local_width // HEAD_DIM
    tiles = ctx * rows // HEAD_DIM
    mask_rows = rows // BLOCK * tiles
    smem = pl.BlockSpec(memory_space=pltpu.SMEM)
    vmem = pl.BlockSpec(memory_space=pltpu.VMEM)
    anywhere = pl.BlockSpec(memory_space=pl.ANY)
    room = pltpu.CompilerParams(vmem_limit_bytes=8 << 20)
    def far_piece(flip):
        seq = (me[0] ^ flip) % seqs
        take = lambda block: lax.dynamic_slice_in_dim(block, seq, 1, 0)[0]
        return jnp.concatenate([take(keys), take(values)], 0)

    sent = [far_piece(flip) for flip in FAR]
    own, *asked = pl.pallas_call(
        functools.partial(count_kernel, ctx=ctx),
        in_specs=[smem] * 4,
        out_specs=[vmem] * seqs,
        out_shape=[jax.ShapeDtypeStruct((mask_rows, HEAD_DIM), jnp.bfloat16)] * seqs,
        compiler_params=room,
        name="count",
    )(me, global_ids.T, rand_ids, rand_count.T)
    packed = jnp.concatenate([queries, keys, values], 1)
    got = {
        flip: lax.ppermute(part, "ctx", [(i, i ^ flip) for i in range(ctx)])
        for flip, part in zip(FAR, sent)
    }
    halves = [[half * seqs + c for c in range(seqs)] for half in range(ctx // seqs)]
    near = lax.all_to_all(packed, "ctx", split_axis=0, concat_axis=0, tiled=True, axis_index_groups=halves)
    counts = [own] + [
        lax.ppermute(part, "ctx", [(i, i ^ (n + 1)) for i in range(ctx)]) for n, part in enumerate(asked)
    ]
    early = pl.pallas_call(
        stack_kernel,
        in_specs=[vmem] * len(EARLY),
        out_specs=vmem,
        out_shape=jax.ShapeDtypeStruct((len(EARLY), 2 * rows, local_width), jnp.bfloat16),
        compiler_params=room,
        cost_estimate=pl.CostEstimate(flops=9 * 10**9, bytes_accessed=0, transcendentals=0),
        name="stack",
    )(*[got[flip] for flip in EARLY])
    late = [got[flip] for flip in LATE]
    pairs = heads * seqs * rows * ctx * rows
    cost = pl.CostEstimate(
        flops=2 * pairs * HEAD_DIM, bytes_accessed=2 * pairs, transcendentals=pairs
    )
    weights = pl.pallas_call(
        functools.partial(weigh_kernel, rows=rows, tiles=tiles, late=len(late)),
        in_specs=[smem] + [vmem] * (2 + len(late) + seqs),
        out_specs=vmem,
        out_shape=jax.ShapeDtypeStruct((seqs * heads, rows, ctx * rows), jnp.bfloat16),
        compiler_params=room,
        cost_estimate=cost,
        name="weigh",
    )(me, near, early, *late, *counts)
    sides = 2
    attention = pl.pallas_call(
        functools.partial(sum_kernel, copies=sides),
        in_specs=[smem] + [vmem] * (3 + len(late)),
        out_specs=vmem,
        out_shape=jax.ShapeDtypeStruct((seqs * sides, rows, local_width), jnp.bfloat16),
        compiler_params=room,
        cost_estimate=cost,
        name="sum",
    )(me, weights, near, early, *late)
    cores = groups // sides
    home = lax.all_to_all(
        attention,
        ("ctx", "head"),
        split_axis=0,
        concat_axis=0,
        tiled=True,
        axis_index_groups=[
            [(half * seqs + c) * groups + side * cores + core for c in range(seqs) for side in range(sides)]
            for half in range(ctx // seqs)
            for core in range(cores)
        ],
    )
    beside = lax.ppermute(home, "head", [(i, i ^ 1) for i in range(groups)])
    width = out_weight.shape[1]

    def project(flip, dtype, *parts):
        return pl.pallas_call(
            functools.partial(project_kernel, flip=flip),
            in_specs=[smem] + [vmem] * (len(parts) + 1),
            out_specs=vmem,
            out_shape=jax.ShapeDtypeStruct((seqs, rows, width), dtype),
            compiler_params=room,
            cost_estimate=pl.CostEstimate(
                flops=seqs * rows * width * out_weight.shape[0],
                bytes_accessed=4 * seqs * rows * width,
                transcendentals=0,
            ),
            name="project",
        )(group, *parts, out_weight)

    return pl.pallas_call(
        functools.partial(finish_kernel, flip=1, first=0),
        in_specs=[smem] + [vmem] * 3,
        out_specs=anywhere,
        out_shape=jax.ShapeDtypeStruct((seqs, rows, width), jnp.bfloat16),
        scratch_shapes=[
            pltpu.VMEM((seqs, rows, width), jnp.bfloat16),
            pltpu.SemaphoreType.DMA((seqs,)),
        ],
        compiler_params=room,
        name="finish",
    )(group, project(0, jnp.float32, home), beside, out_weight)


def on_device(queries, keys, values, out_weight, global_ids, rand_ids, rand_count):
    seqs, rows, local_width = queries.shape
    ctx, groups = lax.axis_size("ctx"), lax.axis_size("head")
    fits = ctx == 2 * seqs == 8 and groups == 4 and rows == HEAD_DIM == 2 * BLOCK
    path = half_path if fits else general_path
    return path(queries, keys, values, out_weight, global_ids, rand_ids, rand_count)


def solution(mesh):
    placed = (
        P(None, "ctx", "head"),
        P(None, "ctx", "head"),
        P(None, "ctx", "head"),
        P(None, "head"),
        P(),
        P(None, "ctx", None),
        P(None, "ctx"),
    )
    return jax.shard_map(
        on_device, mesh=mesh, in_specs=placed, out_specs=P(None, "ctx", "head"), check_vma=False
    )
```

```python
import functools

import jax
import jax.numpy as jnp
from jax import lax
from jax.experimental import pallas as pl
from jax.experimental.pallas import tpu as pltpu
from jax.sharding import PartitionSpec as P

HEAD_DIM = 128
BLOCK = 64
GLOB = 2
RMAX = 4


def with_halo(cells, sides, width):
    for axis, dim in sides:
        count = lax.axis_size(axis)
        head = lax.slice_in_dim(cells, 0, width, axis=dim)
        tail = lax.slice_in_dim(cells, cells.shape[dim] - width, cells.shape[dim], axis=dim)
        cells = jnp.concatenate(
            [
                lax.ppermute(tail, axis, [(i, (i + 1) % count) for i in range(count)]),
                cells,
                lax.ppermute(head, axis, [((i + 1) % count, i) for i in range(count)]),
            ],
            axis=dim,
        )
    return cells


def slot_table(slot_of, live_flat, slot_total):
    return (
        (slot_of[:, None] == jnp.arange(slot_total, dtype=jnp.int32)[None, :]) & live_flat[:, None]
    ).astype(jnp.int32)


def general_path(queries, keys, values, out_weight, global_ids, rand_ids, rand_count):
    seq_count, seq_rows, local_width = queries.shape
    blocks_here = seq_rows // BLOCK
    heads_here = local_width // HEAD_DIM
    cycle_size = lax.axis_size("ctx")
    my_index = lax.axis_index("ctx")
    request_count = seq_count * blocks_here * RMAX
    capacity = (request_count + cycle_size - 1) // cycle_size
    slot_total = cycle_size * capacity
    key_width = 3 + GLOB + RMAX
    score_scale = HEAD_DIM ** (-0.5)
    token_pairs = jnp.stack([keys, values], 0)
    block_pairs = jnp.stack(
        [
            keys.reshape(seq_count, blocks_here, BLOCK, local_width),
            values.reshape(seq_count, blocks_here, BLOCK, local_width),
        ],
        2,
    ).reshape(seq_count * blocks_here, 2, BLOCK, local_width)
    extended = with_halo(token_pairs, (("ctx", 2),), BLOCK)
    own_blocks = token_pairs.reshape(2, seq_count, blocks_here, BLOCK, local_width)
    shared_owner = global_ids // blocks_here
    shared_local = global_ids % blocks_here
    picker = (
        (shared_local[:, :, None] == jnp.arange(blocks_here, dtype=jnp.int32)[None, None, :])
        & (shared_owner == my_index)[:, :, None]
    ).astype(jnp.bfloat16)
    contribution = jnp.einsum(
        "sgj,xsjtf->xsgtf", picker, own_blocks, preferred_element_type=jnp.float32
    )
    shared_rows = lax.psum(contribution, "ctx").astype(jnp.bfloat16)
    slot_ids = jnp.arange(RMAX, dtype=jnp.int32)
    live_flat = (slot_ids[None, None, :] < rand_count[:, :, None]).reshape(-1)
    owners = (rand_ids // blocks_here).reshape(-1)
    seq_of = jnp.arange(seq_count, dtype=jnp.int32)[:, None, None]
    block_codes = (seq_of * blocks_here + rand_ids % blocks_here).reshape(-1)
    hit_owner = (
        (owners[:, None] == jnp.arange(cycle_size, dtype=jnp.int32)[None, :]) & live_flat[:, None]
    ).astype(jnp.int32)
    rank_within = jnp.sum((jnp.cumsum(hit_owner, axis=0) - hit_owner) * hit_owner, axis=1)
    slot_of = jnp.where(live_flat, owners * capacity + rank_within, 0)
    slot_hits = slot_table(slot_of, live_flat, slot_total)
    requests_out = (jnp.sum(slot_hits * (block_codes[:, None] + 1), axis=0) - 1).reshape(
        cycle_size, capacity
    )
    wanted_here = lax.all_to_all(requests_out, "ctx", split_axis=0, concat_axis=0, tiled=True)
    beside_all = extended.reshape(2, seq_count, blocks_here + 2, BLOCK, local_width)
    window_keys = jnp.stack(
        [beside_all[:, :, offset : offset + blocks_here] for offset in range(3)], 3
    )
    shared_wide = jnp.broadcast_to(
        shared_rows[:, :, None], (2, seq_count, blocks_here, GLOB, BLOCK, local_width)
    )
    local_keys = jnp.concatenate([window_keys, shared_wide], 3)
    query_view = queries.reshape(seq_count, blocks_here, BLOCK, heads_here, HEAD_DIM)
    payload = jnp.take(block_pairs, jnp.maximum(wanted_here, 0).reshape(-1), axis=0).reshape(
        cycle_size, capacity, 2, BLOCK, local_width
    )
    received = lax.all_to_all(payload, "ctx", split_axis=0, concat_axis=0, tiled=True)
    random_rows = jnp.take(received.reshape(slot_total, 2, BLOCK, local_width), slot_of, axis=0)
    random_rows = jnp.moveaxis(
        random_rows.reshape(seq_count, blocks_here, RMAX, 2, BLOCK, local_width), 3, 0
    )
    all_keys = jnp.concatenate([local_keys, random_rows], 3).reshape(
        2, seq_count, blocks_here, key_width * BLOCK, heads_here, HEAD_DIM
    )
    scores = (
        jnp.einsum(
            "sjqhd,sjkhd->sjhqk", query_view, all_keys[0], preferred_element_type=jnp.float32
        )
        * score_scale
    )
    live_slots = jnp.concatenate(
        [
            jnp.ones((seq_count, blocks_here, 3 + GLOB), jnp.bool_),
            slot_ids[None, None, :] < rand_count[:, :, None],
        ],
        2,
    )
    live_cols = jnp.repeat(live_slots, BLOCK, axis=2)[:, :, None, None, :]
    masked = jnp.where(live_cols, scores, -1e30)
    row_peak = jnp.max(masked, axis=-1, keepdims=True)
    weights = jnp.where(live_cols, jnp.exp(masked - row_peak), 0.0)
    row_total = jnp.sum(weights, axis=-1)
    weighted = jnp.einsum(
        "sjhqk,sjkhd->sjqhd",
        weights.astype(jnp.bfloat16),
        all_keys[1],
        preferred_element_type=jnp.float32,
    )
    attention = (
        (weighted / jnp.moveaxis(row_total, 2, 3)[..., None])
        .astype(jnp.bfloat16)
        .reshape(seq_count, seq_rows, local_width)
    )
    projected = jnp.einsum(
        "stf,fo->sto",
        lax.all_gather(attention, "head", axis=2, tiled=True),
        out_weight,
        preferred_element_type=jnp.float32,
    )
    return projected.astype(jnp.bfloat16)


NEAR = (1, 2, 3)
FAR = (4, 5, 6, 7)
EARLY, LATE = FAR, ()


def count_kernel(me_ref, glob_ref, rand_ref, count_ref, *outs, ctx):
    seqs = rand_ref.shape[0]
    blocks_here = rand_ref.shape[1]
    mask_rows = outs[0].shape[0]
    tiles = mask_rows // blocks_here
    blocks = ctx * blocks_here
    me = me_ref[0]
    base = me - lax.rem(me, seqs)
    tile = lax.broadcasted_iota(jnp.int32, (tiles, HEAD_DIM), 0)
    lane = lax.broadcasted_iota(jnp.int32, (tiles, HEAD_DIM), 1)
    for flip, out in enumerate(outs):
        asker = me ^ flip
        seq = lax.rem(asker, seqs)
        holder = jnp.where(tile < seqs, base + tile, asker ^ tile)
        key_block = (holder * HEAD_DIM + lane) // BLOCK
        counts = []
        for j in range(blocks_here):
            block = me * blocks_here + j
            listed = [lax.rem(block + blocks - 1, blocks), block, lax.rem(block + 1, blocks)]
            listed += [glob_ref[g, seq] for g in range(GLOB)]
            listed += [
                jnp.where(r < count_ref[j, seq], rand_ref[seq, j, r], -1) for r in range(RMAX)
            ]
            counts.append(sum((key_block == one).astype(jnp.float32) for one in listed))
        out[...] = jnp.concatenate(counts, 0).astype(jnp.bfloat16)


def stack_kernel(*refs):
    *parts, out_ref = refs
    for n, part in enumerate(parts):
        out_ref[n] = part[...]


def pieces_of(near_ref, early_ref, late_refs):
    pieces = [near_ref.at[n] for n in range(near_ref.shape[0])]
    return pieces + [early_ref.at[n] for n in range(early_ref.shape[0])] + list(late_refs)


def weigh_kernel(me_ref, near_ref, early_ref, *refs, rows, tiles, late):
    *refs, weights_ref = refs
    late_refs, counts_refs = refs[:late], refs[late:]
    pieces = pieces_of(near_ref, early_ref, late_refs)
    askers, _, width = near_ref.shape
    spot = lax.rem(me_ref[0], askers)
    blocks_here = rows // BLOCK
    heads = width // HEAD_DIM
    scale = HEAD_DIM ** (-0.5) * 1.4426950408889634
    biases = []
    for n in range(askers):
        counts = counts_refs[n][...].astype(jnp.float32)
        biases.append(jnp.where(counts > 0, jnp.log2(jnp.maximum(counts, 1.0)), -1e30))
    for h in range(heads):
        cols = slice(h * HEAD_DIM, (h + 1) * HEAD_DIM)
        keys = [ref[ref.shape[0] - 2 * rows : ref.shape[0] - rows, cols] for ref in pieces]
        scores = lax.dot_general(
            jnp.concatenate([near_ref[spot ^ n, 0:rows, cols] for n in range(askers)], 0),
            jnp.concatenate(keys, 0),
            (((1,), (1,)), ((), ())),
            preferred_element_type=jnp.float32,
        )
        for n in range(askers):
            for j in range(blocks_here):
                at = n * rows + j * BLOCK
                wide = jnp.concatenate(
                    [biases[n][j * tiles + i : j * tiles + i + 1, :] for i in tuple(range(askers)) + FAR], 1
                )
                shifted = scores[at : at + BLOCK] * scale + wide
                weights = jnp.exp2(shifted - jnp.max(shifted, axis=1, keepdims=True))
                weights_ref[n * heads + h, j * BLOCK : (j + 1) * BLOCK, :] = weights.astype(jnp.bfloat16)


def sum_kernel(me_ref, weights_ref, near_ref, early_ref, *refs, copies):
    *late_refs, out_ref = refs
    pieces = pieces_of(near_ref, early_ref, late_refs)
    count, rows, span = weights_ref.shape
    spot = lax.rem(me_ref[0], near_ref.shape[0])
    heads = near_ref.shape[2] // HEAD_DIM
    ones = jnp.ones((span, HEAD_DIM), jnp.bfloat16)
    for h in range(heads):
        cols = slice(h * HEAD_DIM, (h + 1) * HEAD_DIM)
        values = jnp.concatenate([ref[ref.shape[0] - rows :, cols] for ref in pieces], 0)
        both = jnp.concatenate([values, ones], 1)
        for n in range(count // heads):
            sums = jnp.dot(weights_ref[n * heads + h], both, preferred_element_type=jnp.float32)
            result = (sums[:, :HEAD_DIM] / sums[:, HEAD_DIM:]).astype(jnp.bfloat16)
            for copy in range(copies):
                out_ref[(spot ^ n) * copies + copy, :, cols] = result


def project_kernel(group_ref, *refs, flip):
    *before, part_ref, weight_ref, out_ref = refs
    slots, rows, depth = part_ref.shape
    seqs = out_ref.shape[0]
    sides = slots // seqs
    cores = weight_ref.shape[0] // (depth * sides)
    core = lax.rem(group_ref[0], cores) ^ flip
    weights = [
        weight_ref[pl.ds(pl.multiple_of((side * cores + core) * depth, depth), depth), :]
        for side in range(sides)
    ]
    for seq in range(seqs):
        total = before[0][seq] if before else 0.0
        for side in range(sides):
            total = total + jnp.dot(
                part_ref[seq * sides + side], weights[side], preferred_element_type=jnp.float32
            )
        out_ref[seq] = total.astype(out_ref.dtype)


def finish_kernel(group_ref, before_ref, part_ref, weight_ref, *refs, flip, first):
    *_, out_ref, buffer, sems = refs
    slots, rows, depth = part_ref.shape
    sides = slots // buffer.shape[0]
    cores = weight_ref.shape[0] // (depth * sides)
    core = lax.rem(group_ref[0], cores) ^ flip
    weights = [
        weight_ref[pl.ds(pl.multiple_of((side * cores + core) * depth, depth), depth), :]
        for side in range(sides)
    ]
    weight = jnp.concatenate(weights, 0)
    copies = []
    for n in range(buffer.shape[0]):
        features = jnp.concatenate([part_ref[n * sides + side] for side in range(sides)], 1)
        total = before_ref[first + n] + jnp.dot(features, weight, preferred_element_type=jnp.float32)
        buffer[n] = total.astype(buffer.dtype)
        copies.append(pltpu.make_async_copy(buffer.at[n], out_ref.at[first + n], sems.at[n]))
        copies[-1].start()
    for copy in copies:
        copy.wait()


def half_path(queries, keys, values, out_weight, global_ids, rand_ids, rand_count):
    seqs, rows, local_width = queries.shape
    ctx = lax.axis_size("ctx")
    groups = lax.axis_size("head")
    me = lax.axis_index("ctx").astype(jnp.int32).reshape(1)
    group = lax.axis_index("head").astype(jnp.int32).reshape(1)
    heads = local_width // HEAD_DIM
    tiles = ctx * rows // HEAD_DIM
    mask_rows = rows // BLOCK * tiles
    smem = pl.BlockSpec(memory_space=pltpu.SMEM)
    vmem = pl.BlockSpec(memory_space=pltpu.VMEM)
    anywhere = pl.BlockSpec(memory_space=pl.ANY)
    room = pltpu.CompilerParams(vmem_limit_bytes=8 << 20)
    def far_piece(flip):
        seq = (me[0] ^ flip) % seqs
        take = lambda block: lax.dynamic_slice_in_dim(block, seq, 1, 0)[0]
        return jnp.concatenate([take(keys), take(values)], 0)

    sent = [far_piece(flip) for flip in FAR]
    own, *asked = pl.pallas_call(
        functools.partial(count_kernel, ctx=ctx),
        in_specs=[smem] * 4,
        out_specs=[vmem] * seqs,
        out_shape=[jax.ShapeDtypeStruct((mask_rows, HEAD_DIM), jnp.bfloat16)] * seqs,
        compiler_params=room,
        name="count",
    )(me, global_ids.T, rand_ids, rand_count.T)
    packed = jnp.concatenate([queries, keys, values], 1)
    got = {
        flip: lax.ppermute(part, "ctx", [(i, i ^ flip) for i in range(ctx)])
        for flip, part in zip(FAR, sent)
    }
    halves = [[half * seqs + c for c in range(seqs)] for half in range(ctx // seqs)]
    near = lax.all_to_all(packed, "ctx", split_axis=0, concat_axis=0, tiled=True, axis_index_groups=halves)
    counts = [own] + [
        lax.ppermute(part, "ctx", [(i, i ^ (n + 1)) for i in range(ctx)]) for n, part in enumerate(asked)
    ]
    early = pl.pallas_call(
        stack_kernel,
        in_specs=[vmem] * len(EARLY),
        out_specs=vmem,
        out_shape=jax.ShapeDtypeStruct((len(EARLY), 2 * rows, local_width), jnp.bfloat16),
        compiler_params=room,
        cost_estimate=pl.CostEstimate(flops=9 * 10**9, bytes_accessed=0, transcendentals=0),
        name="stack",
    )(*[got[flip] for flip in EARLY])
    late = [got[flip] for flip in LATE]
    pairs = heads * seqs * rows * ctx * rows
    cost = pl.CostEstimate(
        flops=2 * pairs * HEAD_DIM, bytes_accessed=2 * pairs, transcendentals=pairs
    )
    weights = pl.pallas_call(
        functools.partial(weigh_kernel, rows=rows, tiles=tiles, late=len(late)),
        in_specs=[smem] + [vmem] * (2 + len(late) + seqs),
        out_specs=vmem,
        out_shape=jax.ShapeDtypeStruct((seqs * heads, rows, ctx * rows), jnp.bfloat16),
        compiler_params=room,
        cost_estimate=cost,
        name="weigh",
    )(me, near, early, *late, *counts)
    sides = 2
    attention = pl.pallas_call(
        functools.partial(sum_kernel, copies=sides),
        in_specs=[smem] + [vmem] * (3 + len(late)),
        out_specs=vmem,
        out_shape=jax.ShapeDtypeStruct((seqs * sides, rows, local_width), jnp.bfloat16),
        compiler_params=room,
        cost_estimate=cost,
        name="sum",
    )(me, weights, near, early, *late)
    cores = groups // sides
    home = lax.all_to_all(
        attention,
        ("ctx", "head"),
        split_axis=0,
        concat_axis=0,
        tiled=True,
        axis_index_groups=[
            [(half * seqs + c) * groups + side * cores + core for c in range(seqs) for side in range(sides)]
            for half in range(ctx // seqs)
            for core in range(cores)
        ],
    )
    beside = lax.ppermute(home, "head", [(i, i ^ 1) for i in range(groups)])
    width = out_weight.shape[1]

    def project(flip, dtype, *parts):
        return pl.pallas_call(
            functools.partial(project_kernel, flip=flip),
            in_specs=[smem] + [vmem] * (len(parts) + 1),
            out_specs=vmem,
            out_shape=jax.ShapeDtypeStruct((seqs, rows, width), dtype),
            compiler_params=room,
            cost_estimate=pl.CostEstimate(
                flops=seqs * rows * width * out_weight.shape[0],
                bytes_accessed=4 * seqs * rows * width,
                transcendentals=0,
            ),
            name="project",
        )(group, *parts, out_weight)

    return pl.pallas_call(
        functools.partial(finish_kernel, flip=1, first=0),
        in_specs=[smem] + [vmem] * 3,
        out_specs=anywhere,
        out_shape=jax.ShapeDtypeStruct((seqs, rows, width), jnp.bfloat16),
        scratch_shapes=[
            pltpu.VMEM((seqs, rows, width), jnp.bfloat16),
            pltpu.SemaphoreType.DMA((seqs,)),
        ],
        compiler_params=room,
        name="finish",
    )(group, project(0, jnp.float32, home), beside, out_weight)


def on_device(queries, keys, values, out_weight, global_ids, rand_ids, rand_count):
    seqs, rows, local_width = queries.shape
    ctx, groups = lax.axis_size("ctx"), lax.axis_size("head")
    fits = ctx == 2 * seqs == 8 and groups == 4 and rows == HEAD_DIM == 2 * BLOCK
    path = half_path if fits else general_path
    return path(queries, keys, values, out_weight, global_ids, rand_ids, rand_count)


def solution(mesh):
    placed = (
        P(None, "ctx", "head"),
        P(None, "ctx", "head"),
        P(None, "ctx", "head"),
        P(None, "head"),
        P(),
        P(None, "ctx", None),
        P(None, "ctx"),
    )
    return jax.shard_map(
        on_device, mesh=mesh, in_specs=placed, out_specs=P(None, "ctx", "head"), check_vma=False
    )
```

```python
import functools

import jax
import jax.numpy as jnp
from jax import lax
from jax.experimental import pallas as pl
from jax.experimental.pallas import tpu as pltpu
from jax.sharding import PartitionSpec as P

HEAD_DIM = 128
BLOCK = 64
GLOB = 2
RMAX = 4


def with_halo(cells, sides, width):
    for axis, dim in sides:
        count = lax.axis_size(axis)
        head = lax.slice_in_dim(cells, 0, width, axis=dim)
        tail = lax.slice_in_dim(cells, cells.shape[dim] - width, cells.shape[dim], axis=dim)
        cells = jnp.concatenate(
            [
                lax.ppermute(tail, axis, [(i, (i + 1) % count) for i in range(count)]),
                cells,
                lax.ppermute(head, axis, [((i + 1) % count, i) for i in range(count)]),
            ],
            axis=dim,
        )
    return cells


def slot_table(slot_of, live_flat, slot_total):
    return (
        (slot_of[:, None] == jnp.arange(slot_total, dtype=jnp.int32)[None, :]) & live_flat[:, None]
    ).astype(jnp.int32)


def general_path(queries, keys, values, out_weight, global_ids, rand_ids, rand_count):
    seq_count, seq_rows, local_width = queries.shape
    blocks_here = seq_rows // BLOCK
    heads_here = local_width // HEAD_DIM
    cycle_size = lax.axis_size("ctx")
    my_index = lax.axis_index("ctx")
    request_count = seq_count * blocks_here * RMAX
    capacity = (request_count + cycle_size - 1) // cycle_size
    slot_total = cycle_size * capacity
    key_width = 3 + GLOB + RMAX
    score_scale = HEAD_DIM ** (-0.5)
    token_pairs = jnp.stack([keys, values], 0)
    block_pairs = jnp.stack(
        [
            keys.reshape(seq_count, blocks_here, BLOCK, local_width),
            values.reshape(seq_count, blocks_here, BLOCK, local_width),
        ],
        2,
    ).reshape(seq_count * blocks_here, 2, BLOCK, local_width)
    extended = with_halo(token_pairs, (("ctx", 2),), BLOCK)
    own_blocks = token_pairs.reshape(2, seq_count, blocks_here, BLOCK, local_width)
    shared_owner = global_ids // blocks_here
    shared_local = global_ids % blocks_here
    picker = (
        (shared_local[:, :, None] == jnp.arange(blocks_here, dtype=jnp.int32)[None, None, :])
        & (shared_owner == my_index)[:, :, None]
    ).astype(jnp.bfloat16)
    contribution = jnp.einsum(
        "sgj,xsjtf->xsgtf", picker, own_blocks, preferred_element_type=jnp.float32
    )
    shared_rows = lax.psum(contribution, "ctx").astype(jnp.bfloat16)
    slot_ids = jnp.arange(RMAX, dtype=jnp.int32)
    live_flat = (slot_ids[None, None, :] < rand_count[:, :, None]).reshape(-1)
    owners = (rand_ids // blocks_here).reshape(-1)
    seq_of = jnp.arange(seq_count, dtype=jnp.int32)[:, None, None]
    block_codes = (seq_of * blocks_here + rand_ids % blocks_here).reshape(-1)
    hit_owner = (
        (owners[:, None] == jnp.arange(cycle_size, dtype=jnp.int32)[None, :]) & live_flat[:, None]
    ).astype(jnp.int32)
    rank_within = jnp.sum((jnp.cumsum(hit_owner, axis=0) - hit_owner) * hit_owner, axis=1)
    slot_of = jnp.where(live_flat, owners * capacity + rank_within, 0)
    slot_hits = slot_table(slot_of, live_flat, slot_total)
    requests_out = (jnp.sum(slot_hits * (block_codes[:, None] + 1), axis=0) - 1).reshape(
        cycle_size, capacity
    )
    wanted_here = lax.all_to_all(requests_out, "ctx", split_axis=0, concat_axis=0, tiled=True)
    beside_all = extended.reshape(2, seq_count, blocks_here + 2, BLOCK, local_width)
    window_keys = jnp.stack(
        [beside_all[:, :, offset : offset + blocks_here] for offset in range(3)], 3
    )
    shared_wide = jnp.broadcast_to(
        shared_rows[:, :, None], (2, seq_count, blocks_here, GLOB, BLOCK, local_width)
    )
    local_keys = jnp.concatenate([window_keys, shared_wide], 3)
    query_view = queries.reshape(seq_count, blocks_here, BLOCK, heads_here, HEAD_DIM)
    payload = jnp.take(block_pairs, jnp.maximum(wanted_here, 0).reshape(-1), axis=0).reshape(
        cycle_size, capacity, 2, BLOCK, local_width
    )
    received = lax.all_to_all(payload, "ctx", split_axis=0, concat_axis=0, tiled=True)
    random_rows = jnp.take(received.reshape(slot_total, 2, BLOCK, local_width), slot_of, axis=0)
    random_rows = jnp.moveaxis(
        random_rows.reshape(seq_count, blocks_here, RMAX, 2, BLOCK, local_width), 3, 0
    )
    all_keys = jnp.concatenate([local_keys, random_rows], 3).reshape(
        2, seq_count, blocks_here, key_width * BLOCK, heads_here, HEAD_DIM
    )
    scores = (
        jnp.einsum(
            "sjqhd,sjkhd->sjhqk", query_view, all_keys[0], preferred_element_type=jnp.float32
        )
        * score_scale
    )
    live_slots = jnp.concatenate(
        [
            jnp.ones((seq_count, blocks_here, 3 + GLOB), jnp.bool_),
            slot_ids[None, None, :] < rand_count[:, :, None],
        ],
        2,
    )
    live_cols = jnp.repeat(live_slots, BLOCK, axis=2)[:, :, None, None, :]
    masked = jnp.where(live_cols, scores, -1e30)
    row_peak = jnp.max(masked, axis=-1, keepdims=True)
    weights = jnp.where(live_cols, jnp.exp(masked - row_peak), 0.0)
    row_total = jnp.sum(weights, axis=-1)
    weighted = jnp.einsum(
        "sjhqk,sjkhd->sjqhd",
        weights.astype(jnp.bfloat16),
        all_keys[1],
        preferred_element_type=jnp.float32,
    )
    attention = (
        (weighted / jnp.moveaxis(row_total, 2, 3)[..., None])
        .astype(jnp.bfloat16)
        .reshape(seq_count, seq_rows, local_width)
    )
    projected = jnp.einsum(
        "stf,fo->sto",
        lax.all_gather(attention, "head", axis=2, tiled=True),
        out_weight,
        preferred_element_type=jnp.float32,
    )
    return projected.astype(jnp.bfloat16)


NEAR = (1, 2, 3)
FAR = (4, 5, 6, 7)
EARLY, LATE = FAR, ()


def count_kernel(me_ref, glob_ref, rand_ref, count_ref, *outs, ctx):
    seqs = rand_ref.shape[0]
    blocks_here = rand_ref.shape[1]
    mask_rows = outs[0].shape[0]
    tiles = mask_rows // blocks_here
    blocks = ctx * blocks_here
    me = me_ref[0]
    base = me - lax.rem(me, seqs)
    tile = lax.broadcasted_iota(jnp.int32, (tiles, HEAD_DIM), 0)
    lane = lax.broadcasted_iota(jnp.int32, (tiles, HEAD_DIM), 1)
    for flip, out in enumerate(outs):
        asker = me ^ flip
        seq = lax.rem(asker, seqs)
        holder = jnp.where(tile < seqs, base + tile, asker ^ tile)
        key_block = (holder * HEAD_DIM + lane) // BLOCK
        counts = []
        for j in range(blocks_here):
            block = me * blocks_here + j
            listed = [lax.rem(block + blocks - 1, blocks), block, lax.rem(block + 1, blocks)]
            listed += [glob_ref[g, seq] for g in range(GLOB)]
            listed += [
                jnp.where(r < count_ref[j, seq], rand_ref[seq, j, r], -1) for r in range(RMAX)
            ]
            counts.append(sum((key_block == one).astype(jnp.float32) for one in listed))
        out[...] = jnp.concatenate(counts, 0).astype(jnp.bfloat16)


def stack_kernel(*refs):
    *parts, out_ref = refs
    for n, part in enumerate(parts):
        out_ref[n] = part[...]


def pieces_of(near_ref, early_ref, late_refs):
    pieces = [near_ref.at[n] for n in range(near_ref.shape[0])]
    return pieces + [early_ref.at[n] for n in range(early_ref.shape[0])] + list(late_refs)


def weigh_kernel(me_ref, near_ref, early_ref, *refs, rows, tiles, late):
    *refs, weights_ref = refs
    late_refs, counts_refs = refs[:late], refs[late:]
    pieces = pieces_of(near_ref, early_ref, late_refs)
    askers, _, width = near_ref.shape
    spot = lax.rem(me_ref[0], askers)
    blocks_here = rows // BLOCK
    heads = width // HEAD_DIM
    scale = HEAD_DIM ** (-0.5) * 1.4426950408889634
    biases = []
    for n in range(askers):
        counts = counts_refs[n][...].astype(jnp.float32)
        biases.append(jnp.where(counts > 0, jnp.log2(jnp.maximum(counts, 1.0)), -1e30))
    for h in range(heads):
        cols = slice(h * HEAD_DIM, (h + 1) * HEAD_DIM)
        keys = [ref[ref.shape[0] - 2 * rows : ref.shape[0] - rows, cols] for ref in pieces]
        scores = lax.dot_general(
            jnp.concatenate([near_ref[spot ^ n, 0:rows, cols] for n in range(askers)], 0),
            jnp.concatenate(keys, 0),
            (((1,), (1,)), ((), ())),
            preferred_element_type=jnp.float32,
        )
        for n in range(askers):
            for j in range(blocks_here):
                at = n * rows + j * BLOCK
                wide = jnp.concatenate(
                    [biases[n][j * tiles + i : j * tiles + i + 1, :] for i in tuple(range(askers)) + FAR], 1
                )
                shifted = scores[at : at + BLOCK] * scale + wide
                weights = jnp.exp2(shifted - jnp.max(shifted, axis=1, keepdims=True))
                weights_ref[h * askers + n, j * BLOCK : (j + 1) * BLOCK, :] = weights.astype(jnp.bfloat16)


def sum_kernel(me_ref, weights_ref, near_ref, early_ref, *refs, copies):
    *late_refs, out_ref = refs
    pieces = pieces_of(near_ref, early_ref, late_refs)
    count, rows, span = weights_ref.shape
    spot = lax.rem(me_ref[0], near_ref.shape[0])
    heads = near_ref.shape[2] // HEAD_DIM
    ones = jnp.ones((span, HEAD_DIM), jnp.bfloat16)
    for h in range(heads):
        cols = slice(h * HEAD_DIM, (h + 1) * HEAD_DIM)
        values = jnp.concatenate([ref[ref.shape[0] - rows :, cols] for ref in pieces], 0)
        both = jnp.concatenate([values, ones], 1)
        asked = count // heads
        left = weights_ref[h * asked : (h + 1) * asked].reshape(asked * rows, span)
        totals = jnp.dot(left, both, preferred_element_type=jnp.float32)
        for n in range(asked):
            sums = totals[n * rows : (n + 1) * rows]
            result = (sums[:, :HEAD_DIM] / sums[:, HEAD_DIM:]).astype(jnp.bfloat16)
            for copy in range(copies):
                out_ref[(spot ^ n) * copies + copy, :, cols] = result


def project_kernel(group_ref, *refs, flip):
    *before, part_ref, weight_ref, out_ref = refs
    slots, rows, depth = part_ref.shape
    seqs = out_ref.shape[0]
    sides = slots // seqs
    cores = weight_ref.shape[0] // (depth * sides)
    core = lax.rem(group_ref[0], cores) ^ flip
    weights = [
        weight_ref[pl.ds(pl.multiple_of((side * cores + core) * depth, depth), depth), :]
        for side in range(sides)
    ]
    for seq in range(seqs):
        total = before[0][seq] if before else 0.0
        for side in range(sides):
            total = total + jnp.dot(
                part_ref[seq * sides + side], weights[side], preferred_element_type=jnp.float32
            )
        out_ref[seq] = total.astype(out_ref.dtype)


def finish_kernel(group_ref, before_ref, part_ref, weight_ref, *refs, flip, first):
    *_, out_ref, buffer, sems = refs
    slots, rows, depth = part_ref.shape
    sides = slots // buffer.shape[0]
    cores = weight_ref.shape[0] // (depth * sides)
    core = lax.rem(group_ref[0], cores) ^ flip
    weights = [
        weight_ref[pl.ds(pl.multiple_of((side * cores + core) * depth, depth), depth), :]
        for side in range(sides)
    ]
    weight = jnp.concatenate(weights, 0)
    copies = []
    for n in range(buffer.shape[0]):
        features = jnp.concatenate([part_ref[n * sides + side] for side in range(sides)], 1)
        total = before_ref[first + n] + jnp.dot(features, weight, preferred_element_type=jnp.float32)
        buffer[n] = total.astype(buffer.dtype)
        copies.append(pltpu.make_async_copy(buffer.at[n], out_ref.at[first + n], sems.at[n]))
        copies[-1].start()
    for copy in copies:
        copy.wait()


def half_path(queries, keys, values, out_weight, global_ids, rand_ids, rand_count):
    seqs, rows, local_width = queries.shape
    ctx = lax.axis_size("ctx")
    groups = lax.axis_size("head")
    me = lax.axis_index("ctx").astype(jnp.int32).reshape(1)
    group = lax.axis_index("head").astype(jnp.int32).reshape(1)
    heads = local_width // HEAD_DIM
    tiles = ctx * rows // HEAD_DIM
    mask_rows = rows // BLOCK * tiles
    smem = pl.BlockSpec(memory_space=pltpu.SMEM)
    vmem = pl.BlockSpec(memory_space=pltpu.VMEM)
    anywhere = pl.BlockSpec(memory_space=pl.ANY)
    room = pltpu.CompilerParams(vmem_limit_bytes=8 << 20)
    def far_piece(flip):
        seq = (me[0] ^ flip) % seqs
        take = lambda block: lax.dynamic_slice_in_dim(block, seq, 1, 0)[0]
        return jnp.concatenate([take(keys), take(values)], 0)

    sent = [far_piece(flip) for flip in FAR]
    own, *asked = pl.pallas_call(
        functools.partial(count_kernel, ctx=ctx),
        in_specs=[smem] * 4,
        out_specs=[vmem] * seqs,
        out_shape=[jax.ShapeDtypeStruct((mask_rows, HEAD_DIM), jnp.bfloat16)] * seqs,
        compiler_params=room,
        name="count",
    )(me, global_ids.T, rand_ids, rand_count.T)
    packed = jnp.concatenate([queries, keys, values], 1)
    got = {
        flip: lax.ppermute(part, "ctx", [(i, i ^ flip) for i in range(ctx)])
        for flip, part in zip(FAR, sent)
    }
    halves = [[half * seqs + c for c in range(seqs)] for half in range(ctx // seqs)]
    near = lax.all_to_all(packed, "ctx", split_axis=0, concat_axis=0, tiled=True, axis_index_groups=halves)
    counts = [own] + [
        lax.ppermute(part, "ctx", [(i, i ^ (n + 1)) for i in range(ctx)]) for n, part in enumerate(asked)
    ]
    early = pl.pallas_call(
        stack_kernel,
        in_specs=[vmem] * len(EARLY),
        out_specs=vmem,
        out_shape=jax.ShapeDtypeStruct((len(EARLY), 2 * rows, local_width), jnp.bfloat16),
        compiler_params=room,
        cost_estimate=pl.CostEstimate(flops=9 * 10**9, bytes_accessed=0, transcendentals=0),
        name="stack",
    )(*[got[flip] for flip in EARLY])
    late = [got[flip] for flip in LATE]
    pairs = heads * seqs * rows * ctx * rows
    cost = pl.CostEstimate(
        flops=2 * pairs * HEAD_DIM, bytes_accessed=2 * pairs, transcendentals=pairs
    )
    weights = pl.pallas_call(
        functools.partial(weigh_kernel, rows=rows, tiles=tiles, late=len(late)),
        in_specs=[smem] + [vmem] * (2 + len(late) + seqs),
        out_specs=vmem,
        out_shape=jax.ShapeDtypeStruct((seqs * heads, rows, ctx * rows), jnp.bfloat16),
        compiler_params=room,
        cost_estimate=cost,
        name="weigh",
    )(me, near, early, *late, *counts)
    sides = 2
    attention = pl.pallas_call(
        functools.partial(sum_kernel, copies=sides),
        in_specs=[smem] + [vmem] * (3 + len(late)),
        out_specs=vmem,
        out_shape=jax.ShapeDtypeStruct((seqs * sides, rows, local_width), jnp.bfloat16),
        compiler_params=room,
        cost_estimate=cost,
        name="sum",
    )(me, weights, near, early, *late)
    cores = groups // sides
    home = lax.all_to_all(
        attention,
        ("ctx", "head"),
        split_axis=0,
        concat_axis=0,
        tiled=True,
        axis_index_groups=[
            [(half * seqs + c) * groups + side * cores + core for c in range(seqs) for side in range(sides)]
            for half in range(ctx // seqs)
            for core in range(cores)
        ],
    )
    beside = lax.ppermute(home, "head", [(i, i ^ 1) for i in range(groups)])
    width = out_weight.shape[1]

    def project(flip, dtype, *parts):
        return pl.pallas_call(
            functools.partial(project_kernel, flip=flip),
            in_specs=[smem] + [vmem] * (len(parts) + 1),
            out_specs=vmem,
            out_shape=jax.ShapeDtypeStruct((seqs, rows, width), dtype),
            compiler_params=room,
            cost_estimate=pl.CostEstimate(
                flops=seqs * rows * width * out_weight.shape[0],
                bytes_accessed=4 * seqs * rows * width,
                transcendentals=0,
            ),
            name="project",
        )(group, *parts, out_weight)

    return pl.pallas_call(
        functools.partial(finish_kernel, flip=1, first=0),
        in_specs=[smem] + [vmem] * 3,
        out_specs=anywhere,
        out_shape=jax.ShapeDtypeStruct((seqs, rows, width), jnp.bfloat16),
        scratch_shapes=[
            pltpu.VMEM((seqs, rows, width), jnp.bfloat16),
            pltpu.SemaphoreType.DMA((seqs,)),
        ],
        compiler_params=room,
        name="finish",
    )(group, project(0, jnp.float32, home), beside, out_weight)


def on_device(queries, keys, values, out_weight, global_ids, rand_ids, rand_count):
    seqs, rows, local_width = queries.shape
    ctx, groups = lax.axis_size("ctx"), lax.axis_size("head")
    fits = ctx == 2 * seqs == 8 and groups == 4 and rows == HEAD_DIM == 2 * BLOCK
    path = half_path if fits else general_path
    return path(queries, keys, values, out_weight, global_ids, rand_ids, rand_count)


def solution(mesh):
    placed = (
        P(None, "ctx", "head"),
        P(None, "ctx", "head"),
        P(None, "ctx", "head"),
        P(None, "head"),
        P(),
        P(None, "ctx", None),
        P(None, "ctx"),
    )
    return jax.shard_map(
        on_device, mesh=mesh, in_specs=placed, out_specs=P(None, "ctx", "head"), check_vma=False
    )
```
